32 devices in a mesh: groups: 2 (over y), row: 4 (over z), col: 4 (over x, core).
Axes of the slice: x: 2, y: 2, z: 4, core: 2. Of those that a mesh axis runs over, the one named last changes fastest.
Arguments:
- inputs: bfloat16 [512, 12288], P(('groups', 'col'), 'row'), parts along dimension 0, may hold values from -6 to 6
- weight: bfloat16 [12288, 24576], P('row', 'col'), may hold values from -0.0546875 to 0.0546875
- cotangent: bfloat16 [512, 24576], P(('groups', 'row'), 'col'), parts along dimension 0, may hold values from -6 to 6
Outputs:
- hidden: bfloat16 [512, 24576], P(('groups', 'row'), 'col'), parts along dimension 0
- grad_inputs: bfloat16 [512, 12288], P(('groups', 'col'), 'row'), parts along dimension 0
- grad_weight: bfloat16 [24576, 24576], P(('groups', 'row'), 'col'), parts along dimension 0
The draws below stay inside these ranges and needn't reach their ends.
There are 2 independent parts, one for each index of `groups`. The reference program is written for one: setup_inputs(seed, part) draws one part's arguments, and reference() takes and returns one part's arrays. A program takes and returns all parts, laid end to end along the dimension named above; an argument that names none is the same for every part. Nothing has to cross between parts.
All inputs are finite; a program needn't handle non-finite values.
Results may differ from the reference program's by a relative error of at most 0.014.
Values may be sent and summed in bfloat16 or wider, within the bound.
No kernel may reach another device: no remote copies, remote signals or barrier semaphores. Data moves between devices by JAX's collectives and lax.ppermute only.
A program may use at most 256 MiB of HBM per device.

```python
import jax
import jax.numpy as jnp
from jax import lax

D = 12288
FF = 24576
TOKENS = 256
N_ROW = 4
N_COL = 4


def steps_of(own_key, shape, split, smallest, high):
    level, own = 1.0, jax.random.fold_in(own_key, 6)
    for dim, blocks in split:
        draws = jnp.exp(jax.random.uniform(jax.random.fold_in(own, dim), (blocks,), jnp.float32, smallest / len(split), high / len(split)))
        level = level * jnp.repeat(draws, shape[dim] // blocks).reshape([-1 if axis == dim else 1 for axis in range(len(shape))])
    return level


def centred(rng, shape, scale, reach, split=(), held_as=jnp.bfloat16):
    gain = steps_of(rng, shape, split, -0.22, 0.18) if split else 1.0
    entries = jax.random.normal(rng, shape, jnp.float32) * scale * gain
    return jnp.minimum(jnp.maximum(entries, -reach), reach).astype(held_as)


def setup_inputs(seed: int = 0, part: int = 0) -> dict:
    key_list = jax.random.split(jax.random.key(seed), 4)
    part_keys = jax.random.split(jax.random.fold_in(key_list[3], part), 4)
    inputs = centred(part_keys[0], (TOKENS, D), 1.0, 6.0, ((0, 4), (1, 4)))
    weight = centred(key_list[1], (D, FF), D ** -0.5, 0.0546875, ((0, 4), (1, 4)))
    cotangent = centred(part_keys[2], (TOKENS, FF), 1.0, 6.0, ((0, 4), (1, 4)))
    return {"inputs": inputs, "weight": weight, "cotangent": cotangent}


tanh_scale = 0.7978845608028654
cubic_coef = 0.044715


def gelu_value(preact):
    inner = tanh_scale * (preact + cubic_coef * preact * preact * preact)
    return 0.5 * preact * (1.0 + jnp.tanh(inner))


def gelu_slope(preact):
    inner = tanh_scale * (preact + cubic_coef * preact * preact * preact)
    tangent = jnp.tanh(inner)
    return 0.5 * (1.0 + tangent) + 0.5 * preact * (1.0 - tangent * tangent) * tanh_scale * (1.0 + 3.0 * cubic_coef * preact * preact)


def rounded(value):
    return lax.optimization_barrier(value.astype(jnp.bfloat16)).astype(jnp.float32)


def reference(inputs, weight, cotangent):
    tokens = inputs.shape[0]
    width = D // N_ROW
    input_blocks = inputs.reshape(tokens, N_ROW, width).transpose(1, 0, 2)
    weight_blocks = weight.reshape(N_ROW, width, FF)

    def add_features(total, pair):
        return total + rounded(jnp.dot(pair[0], pair[1], preferred_element_type=jnp.float32)), None

    preact, _ = lax.scan(add_features, jnp.zeros((tokens, FF), jnp.float32), (input_blocks, weight_blocks))
    hidden = gelu_value(preact).astype(jnp.bfloat16)
    delta_grad = (cotangent.astype(jnp.float32) * gelu_slope(preact)).astype(jnp.bfloat16)
    grad_weight = lax.dot_general(inputs, delta_grad, (((0,), (0,)), ((), ())), preferred_element_type=jnp.float32).astype(jnp.bfloat16)
    units = FF // N_COL
    delta_blocks = delta_grad.reshape(tokens, N_COL, units).transpose(1, 0, 2)
    weight_cols = weight.reshape(D, N_COL, units).transpose(1, 0, 2)

    def add_units(total, pair):
        term = lax.dot_general(pair[0], pair[1], (((1,), (1,)), ((), ())), preferred_element_type=jnp.float32)
        return total + rounded(term), None

    grad_sum, _ = lax.scan(add_units, jnp.zeros((tokens, D), jnp.float32), (delta_blocks, weight_cols))
    grad_inputs = grad_sum.astype(jnp.bfloat16)
    return hidden, grad_inputs, grad_weight
```

```python
import functools

import jax
import jax.numpy as jnp
from jax import lax
from jax.experimental import pallas as pl
from jax.experimental.pallas import tpu as pltpu
from jax.sharding import PartitionSpec as P

tanh_scale = 0.7978845608028654
cubic_coef = 0.044715
bf16 = jnp.bfloat16
f32 = jnp.float32
MIB = 1 << 20

CORES = ((0, 1), (1, 0), (2, 3), (3, 2))
ACROSS = ((0, 2), (2, 0), (1, 3), (3, 1))
PLANE = ("row", "col")
HALVES = tuple((4 * row + col, 4 * (row ^ 1) + col) for row in range(4) for col in range(4))
MIDDLE = tuple(
    (4 * row + col, 4 * (3 - row) + col if row in (1, 2) else 4 * row + (col ^ 1))
    for row in range(4)
    for col in range(4)
)

CHUNKS = 3
SPLIT = 2


def gelu_both(preact):
    inner = tanh_scale * (preact + cubic_coef * preact * preact * preact)
    tangent = jnp.tanh(inner)
    value = 0.5 * preact * (1.0 + tangent)
    slope = 0.5 * (1.0 + tangent) + 0.5 * preact * (1.0 - tangent * tangent) * tanh_scale * (
        1.0 + 3.0 * cubic_coef * preact * preact
    )
    return value, slope


def send(value, axis, pairs):
    return lax.ppermute(value, axis, pairs)


def place_of(token_block, row):
    same_half = (token_block // 2) == (row // 2)
    return jnp.where(same_half, token_block ^ row, jnp.where(row < 2, token_block, 3 - token_block))


def params(limit=48):
    return pltpu.CompilerParams(vmem_limit_bytes=limit * MIB)


def cost(flops, bytes_accessed):
    return pl.CostEstimate(flops=int(flops), bytes_accessed=int(bytes_accessed), transcendentals=0)


def whole(*shape):
    return pl.BlockSpec(shape, lambda j: (0,) * len(shape))


def forward_kernel(w_ref, x_ref, *outs):
    outs, token = outs[:-1], outs[-1]
    token[...] = jnp.zeros_like(token)
    sums = jnp.dot(x_ref[...], w_ref[...], preferred_element_type=f32).astype(bf16)
    rows = outs[0].shape[0]
    for k, out in enumerate(outs):
        out[...] = sums[k * rows : (k + 1) * rows]


def forward_first_kernel(w_ref, *refs):
    pieces, outs, x_ref = refs[:4], refs[4:9], refs[9]
    rows = outs[0].shape[0]

    @pl.when(pl.program_id(0) == 0)
    def _():
        row, col = lax.axis_index("row"), lax.axis_index("col")
        for k, piece in enumerate(pieces):
            at = pl.multiple_of(place_of(col ^ k, row) * rows, rows)
            x_ref[pl.ds(at, rows), :] = piece[...]

    forward_kernel(w_ref, x_ref, *outs)


def tile_of(size, start, want):
    tile = want
    while size % tile or start % tile:
        tile //= 2
    return tile


TOKEN = jax.ShapeDtypeStruct((8, 128), f32)


def forward(x, weight, start, size, tokens, parts, dep=None):
    depth = weight.shape[0]
    tile = tile_of(size, start, 512)
    rows = tokens // parts
    first = isinstance(x, tuple)
    out_shape = [jax.ShapeDtypeStruct((rows, size), bf16)] * parts + [TOKEN]
    out_specs = [pl.BlockSpec((rows, tile), lambda j: (0, j))] * parts + [whole(8, 128)]
    if first:
        out_shape.append(jax.ShapeDtypeStruct((tokens, depth), bf16))
        out_specs.append(whole(tokens, depth))
        in_x = [whole(rows, depth)] * parts
    else:
        in_x = [whole(tokens, depth)]
        x = (x,)
    return call(
        forward_first_kernel if first else forward_kernel,
        [weight, *x],
        [pl.BlockSpec((depth, tile), lambda j: (0, start // tile + j))] + in_x,
        dep,
        grid=(size // tile,),
        out_specs=out_specs,
        out_shape=out_shape,
        compiler_params=params(),
        cost_estimate=cost(2 * tokens * depth * size, 2 * depth * size),
        name="forward_sums",
    )


def stack_blocks(refs, all_ref):
    rows = refs[0].shape[0]
    own, near, mid_m, mid_e, far_m, far_e = refs
    row = lax.axis_index("row")
    middle = (row == 1) | (row == 2)
    all_ref[0:rows] = own[...]
    all_ref[rows : 2 * rows] = near[...]

    @pl.when(middle)
    def _():
        all_ref[2 * rows : 3 * rows] = mid_m[...]
        all_ref[3 * rows :] = far_m[...]

    @pl.when(jnp.logical_not(middle))
    def _():
        all_ref[2 * rows : 3 * rows] = mid_e[...]
        all_ref[3 * rows :] = far_e[...]


def grad_weight_kernel(count, x_ref, *refs):
    blocks, out, token, all_ref = refs[:count], refs[-3], refs[-2], refs[-1]
    token[...] = jnp.zeros_like(token)
    if count == 1:
        all_ref = blocks[0]
    else:
        pl.when(pl.program_id(0) == 0)(lambda: stack_blocks(blocks, all_ref))
    x_t = x_ref[...].T
    size = all_ref.shape[1]
    step = tile_of(size, 0, 512)
    for at in range(0, size, step):
        out[:, at : at + step] = jnp.dot(
            x_t, all_ref[:, at : at + step], preferred_element_type=f32
        ).astype(bf16)


def grad_weight_part(x, blocks, total, start, width, lo, hi, dep=None):
    tokens, depth = x.shape
    size = blocks[0].shape[1]
    tile = tile_of(hi - lo, lo, 512)
    count = len(blocks)
    operands = [x, *blocks]
    in_specs = [pl.BlockSpec((tokens, tile), lambda j: (0, lo // tile + j))]
    in_specs += [whole(*b.shape) for b in blocks]
    aliases = {}
    if total is not None:
        operands.append(total)
        in_specs.append(pl.BlockSpec(memory_space=pl.ANY))
        aliases = {len(operands) - 1: 0}
    return call(
        functools.partial(grad_weight_kernel, count),
        operands,
        in_specs,
        dep,
        grid=((hi - lo) // tile,),
        out_specs=[
            pl.BlockSpec((tile, size), lambda j: (lo // tile + j, start // size)),
            whole(8, 128),
        ],
        out_shape=[jax.ShapeDtypeStruct((depth, width), bf16), TOKEN],
        scratch_shapes=[pltpu.VMEM((tokens, size), bf16)],
        input_output_aliases=aliases,
        compiler_params=params(),
        cost_estimate=cost(2 * tokens * (hi - lo) * size, 2 * (hi - lo) * size),
        name="grad_weight_part",
    )


def grad_inputs_kernel(count, has_total, parts, w_ref, *refs):
    blocks, outs = refs[:count], refs[count + has_total : count + has_total + parts]
    token, staged, all_ref = refs[-3:]
    token[...] = jnp.zeros_like(token)
    if count == 1:
        all_ref = blocks[0]
    else:
        pl.when(pl.program_id(0) == 0)(lambda: stack_blocks(blocks, all_ref))
    value = lax.dot_general(
        all_ref[...], w_ref[...], (((1,), (1,)), ((), ())), preferred_element_type=f32
    )
    if has_total:
        value = value + refs[count][...]
    if parts == 1:
        outs[0][...] = value.astype(outs[0].dtype)
        return
    staged[...] = value.astype(bf16)
    row, col = lax.axis_index("row"), lax.axis_index("col")
    rows = outs[0].shape[0]
    for k, out in enumerate(outs):
        at = pl.multiple_of(place_of(col ^ k, row) * rows, rows)
        out[...] = staged[pl.ds(at, rows), :]


def grad_inputs_part(weight, blocks, total, start, tokens, last, parts, lo, hi, dep=None):
    size = blocks[0].shape[1]
    tile = tile_of(hi - lo, lo, 512)
    count = len(blocks)
    operands = [weight, *blocks]
    in_specs = [pl.BlockSpec((tile, size), lambda j: (lo // tile + j, start // size))]
    in_specs += [whole(*b.shape) for b in blocks]
    if total is not None:
        operands.append(total)
        in_specs.append(pl.BlockSpec((tokens, tile), lambda j: (0, j)))
    rows = tokens // parts
    out_type = bf16 if last else f32
    return call(
        functools.partial(grad_inputs_kernel, count, total is not None, parts),
        operands,
        in_specs,
        dep,
        grid=((hi - lo) // tile,),
        out_specs=[pl.BlockSpec((rows, tile), lambda j: (0, j))] * parts + [whole(8, 128)],
        out_shape=[jax.ShapeDtypeStruct((rows, hi - lo), out_type)] * parts + [TOKEN],
        scratch_shapes=[pltpu.VMEM((tokens, tile), bf16), pltpu.VMEM((tokens, size), bf16)],
        compiler_params=params(),
        cost_estimate=cost(2 * tokens * (hi - lo) * size, 2 * (hi - lo) * size),
        name="grad_inputs_part",
    )


def call(kernel, operands, in_specs, dep, **options):
    count = len(operands)

    def ordered(*refs):
        kernel(*refs[:count], *refs[count + 1 :])

    if dep is None:
        return pl.pallas_call(kernel, in_specs=in_specs, **options)(*operands)
    in_specs = [*in_specs, pl.BlockSpec(memory_space=pl.ANY)]
    return pl.pallas_call(ordered, in_specs=in_specs, **options)(*operands, dep)


def combine(name, kernel, operands, outs, dep):
    vmem = pl.BlockSpec(memory_space=pltpu.VMEM)
    like = operands[0]
    moved = sum(o.size * 2 for o in operands)
    return call(
        kernel,
        operands,
        [vmem] * len(operands),
        dep,
        out_specs=[vmem] * outs,
        out_shape=[jax.ShapeDtypeStruct(like.shape, bf16)] * outs,
        compiler_params=params(16),
        cost_estimate=cost(moved, moved),
        name=name,
    )


def at_end():
    row = lax.axis_index("row")
    return (row == 0) | (row == 3)


def pick(out, at_ends, at_middles):
    end = at_end()

    @pl.when(end)
    def _():
        out[...] = at_ends[...]

    @pl.when(jnp.logical_not(end))
    def _():
        out[...] = at_middles[...]


def pass_on_kernel(a, out):
    out[...] = a[...]


def ends_in_kernel(far, mid_m, near_d, out, relay):
    pick(out, far, mid_m)
    relay[...] = near_d[...]


def copy_two_kernel(a, b, out_a, out_b):
    out_a[...] = a[...]
    out_b[...] = b[...]


def far_sum_kernel(mid, far_m, far, far_in, out, out_sum):
    pick(out, mid, far_m)
    out_sum[...] = far[...] + far_in[...]


def far_sum_only_kernel(mid, far, far_in, out, out_sum):
    out[...] = mid[...]
    out_sum[...] = far[...] + far_in[...]


def near_sum_kernel(near, far_sum, mid, mid_in, out, out_sum):
    end = at_end()
    out_sum[...] = mid[...] + mid_in[...]

    @pl.when(end)
    def _():
        out[...] = near[...]

    @pl.when(jnp.logical_not(end))
    def _():
        out[...] = near[...] + far_sum[...]


def gelu_kernel(own, near_sum, mid_sum, cotangent, hidden, delta):
    end = at_end()
    width = own.shape[1]
    step = 256 if width % 256 == 0 else width

    def body(j, carry):
        cols = pl.ds(pl.multiple_of(j * step, step), step)
        from_mid = jnp.where(end, 0.0, mid_sum[:, cols].astype(f32))
        preact = own[:, cols].astype(f32) + from_mid + near_sum[:, cols].astype(f32)
        value, slope = gelu_both(preact)
        hidden[:, cols] = value.astype(bf16)
        delta[:, cols] = (cotangent[:, cols].astype(f32) * slope).astype(bf16)
        return carry

    lax.fori_loop(0, width // step, body, 0)


def gather_inputs(inputs):
    across = send(inputs, "col", ACROSS)
    beside = send(inputs, "col", CORES)
    corner = send(across, "col", CORES)
    return (inputs, beside, across, corner)


def scatter_cols(pieces):
    keep, give, keep_far, give_far = pieces
    far_sum = keep_far + send(give_far, "col", CORES)
    across = send(far_sum, "col", ACROSS)
    near_sum = keep + send(give, "col", CORES)
    return (near_sum.astype(f32) + across.astype(f32)).astype(bf16)


class Work:
    def __init__(self):
        self.queue, self.token = [], None

    def add(self, kernel):
        self.queue.append(kernel)

    def run(self, dep):
        if self.queue:
            self.token = self.queue.pop(0)(dep)

    def step(self, name, kernel, operands, pairs):
        values = combine(name, kernel, operands, len(pairs), self.token)
        arrived = [send(value, PLANE, to) for value, to in zip(values, pairs)]
        self.run(values[0])
        return arrived


def on_line(inputs, weight, cotangent):
    depth, width = weight.shape
    tokens = 4 * inputs.shape[0]
    size = width // CHUNKS
    cuts = [depth * k // SPLIT for k in range(SPLIT + 1)]
    bounds = list(zip(cuts[:-1], cuts[1:]))
    work = Work()
    sums, delta, blocks, hidden = {}, {}, {}, {}
    state = {"total": [None] * SPLIT, "grad_weight": None}

    *sums[0], _, x = forward(gather_inputs(inputs), weight, 0, size, tokens, 4)

    def add_forward(k):
        def run(dep):
            *sums[k], token = forward(x, weight, k * size, size, tokens, 4, dep)
            return token

        work.add(run)

    def add_grads(k):
        def run_inputs(part, dep):
            state["total"][part], token = grad_inputs_part(
                weight, blocks[k], state["total"][part], k * size, tokens, False, 1, *bounds[part], dep
            )
            return token

        def run_weight(part, dep):
            state["grad_weight"], token = grad_weight_part(
                x, blocks[k], state["grad_weight"], k * size, width, *bounds[part], dep
            )
            return token

        for run in (run_inputs, run_weight):
            for part in range(SPLIT):
                work.add(functools.partial(run, part))

    for k in range(CHUNKS + 1):
        summing, gathering = k < CHUNKS, k > 0
        if k + 1 < CHUNKS:
            add_forward(k + 1)
        if gathering:
            near_d = send(delta[k - 1], PLANE, HALVES)
            mid_m = send(delta[k - 1], PLANE, MIDDLE)
            work.run(delta[k - 1])
        if summing:
            own, near, mid, far = sums[k]
        if summing and gathering:
            far_in, far_m = work.step("ends_in", ends_in_kernel, (far, mid_m, near_d), (HALVES, MIDDLE))
            mid_in, far_sum = work.step(
                "far_sum", far_sum_kernel, (mid, far_m, far, far_in), (HALVES, MIDDLE)
            )
            mid_e, far_e = far_in, mid_in
        elif summing:
            far_in = send(far, PLANE, HALVES)
            work.run(far)
            mid_in, far_sum = work.step(
                "far_sum", far_sum_only_kernel, (mid, far, far_in), (HALVES, MIDDLE)
            )
        else:
            mid_e, far_m = work.step("relay", copy_two_kernel, (mid_m, near_d), (HALVES, MIDDLE))
            (far_e,) = work.step("relay_far", pass_on_kernel, (far_m,), (HALVES,))
        if gathering:
            blocks[k - 1] = [delta[k - 1], near_d, mid_m, mid_e, far_m, far_e]
            if summing:
                add_grads(k - 1)
        if summing:
            near_sum, mid_sum = work.step(
                "near_sum", near_sum_kernel, (near, far_sum, mid, mid_in), (HALVES, MIDDLE)
            )
            part = cotangent[:, k * size : (k + 1) * size]
            hidden[k], delta[k] = combine(
                "gelu", gelu_kernel, (own, near_sum, mid_sum, part), 2, work.token
            )
    while work.queue:
        work.run(work.token)
    last = CHUNKS - 1
    halves = []
    for part, (lo, hi) in enumerate(bounds):
        *pieces, work.token = grad_inputs_part(
            weight, blocks[last], state["total"][part], last * size, tokens, True, 4, lo, hi, work.token
        )
        halves.append(scatter_cols(pieces))
    grad_weight, _ = grad_weight_part(
        x, blocks[last], state["grad_weight"], last * size, width, 0, depth, work.token
    )
    return (
        jnp.concatenate([hidden[k] for k in range(CHUNKS)], axis=1),
        jnp.concatenate(halves, axis=1),
        grad_weight,
    )


def on_any(inputs, weight, cotangent):
    depth, width = weight.shape
    x = lax.all_gather(inputs, "col", axis=0, tiled=True)
    tokens = x.shape[0]
    sums, _ = forward(x, weight, 0, width, tokens, 1)
    preact = lax.psum_scatter(sums, "row", scatter_dimension=0, tiled=True).astype(f32)
    value, slope = gelu_both(preact)
    delta = (cotangent.astype(f32) * slope).astype(bf16)
    blocks = [lax.all_gather(delta, "row", axis=0, tiled=True)]
    sums, _ = grad_inputs_part(weight, blocks, None, 0, tokens, True, 1, 0, depth)
    grad_inputs = lax.psum_scatter(sums, "col", scatter_dimension=0, tiled=True)
    grad_weight, _ = grad_weight_part(x, blocks, None, 0, width, 0, depth)
    return (value.astype(bf16), grad_inputs, grad_weight)


def solution(mesh):
    in_specs = (P(("groups", "col"), "row"), P("row", "col"), P(("groups", "row"), "col"))
    out_specs = (
        P(("groups", "row"), "col"),
        P(("groups", "col"), "row"),
        P(("groups", "row"), "col"),
    )
    fits = mesh.shape["row"] == 4 and mesh.shape["col"] == 4
    return jax.shard_map(
        on_line if fits else on_any,
        mesh=mesh,
        in_specs=in_specs,
        out_specs=out_specs,
        check_vma=False,
    )
```

```python
import functools

import jax
import jax.numpy as jnp
from jax import lax
from jax.experimental import pallas as pl
from jax.experimental.pallas import tpu as pltpu
from jax.sharding import PartitionSpec as P

tanh_scale = 0.7978845608028654
cubic_coef = 0.044715
bf16 = jnp.bfloat16
f32 = jnp.float32
MIB = 1 << 20

CORES = ((0, 1), (1, 0), (2, 3), (3, 2))
ACROSS = ((0, 2), (2, 0), (1, 3), (3, 1))
PLANE = ("row", "col")
HALVES = tuple((4 * row + col, 4 * (row ^ 1) + col) for row in range(4) for col in range(4))
MIDDLE = tuple(
    (4 * row + col, 4 * (3 - row) + col if row in (1, 2) else 4 * row + (col ^ 1))
    for row in range(4)
    for col in range(4)
)

STREAMS = 2
ROUNDS = 2
SPLIT = 2


def gelu_both(preact):
    inner = tanh_scale * (preact + cubic_coef * preact * preact * preact)
    tangent = jnp.tanh(inner)
    value = 0.5 * preact * (1.0 + tangent)
    slope = 0.5 * (1.0 + tangent) + 0.5 * preact * (1.0 - tangent * tangent) * tanh_scale * (
        1.0 + 3.0 * cubic_coef * preact * preact
    )
    return value, slope


def send(value, axis, pairs):
    return lax.ppermute(value, axis, pairs)


def place_of(token_block, row):
    same_half = (token_block // 2) == (row // 2)
    return jnp.where(same_half, token_block ^ row, jnp.where(row < 2, token_block, 3 - token_block))


def params(limit=48):
    return pltpu.CompilerParams(vmem_limit_bytes=limit * MIB)


def cost(flops, bytes_accessed):
    return pl.CostEstimate(flops=int(flops), bytes_accessed=int(bytes_accessed), transcendentals=0)


def whole(*shape):
    return pl.BlockSpec(shape, lambda j: (0,) * len(shape))


def resident():
    return pl.BlockSpec(memory_space=pltpu.VMEM)


def tile_of(size, want):
    tile = want
    while size % tile:
        tile //= 2
    return tile


TILE = 512
UNROLL = True
TOKEN = jax.ShapeDtypeStruct((8, 128), f32)


def fetch(source, rows, columns, buffer, sems, tile, by_rows, i):
    at = pl.ds(pl.multiple_of(i * tile, tile), tile)
    if by_rows:
        part = source.at[pl.ds(pl.multiple_of(rows[0] + i * tile, tile), tile), pl.ds(*columns)]
        return pltpu.make_async_copy(part, buffer.at[at, :], sems.at[i])
    part = source.at[pl.ds(*rows), pl.ds(pl.multiple_of(columns[0] + i * tile, tile), tile)]
    return pltpu.make_async_copy(part, buffer.at[:, at], sems.at[i])


def each(count, body):
    def run(i, carry):
        body(i)
        return carry

    lax.fori_loop(0, count, run, 0)


def forward_kernel(start, tile, parts, first, w_ref, *refs):
    *refs, buffer, sems = refs
    depth, size = buffer.shape
    load = functools.partial(fetch, w_ref, (0, depth), (start, size), buffer, sems, tile, False)
    each(size // tile, lambda i: load(i).start())
    if first:
        pieces, outs, token, x_ref = refs[:parts], refs[parts : 2 * parts], refs[-2], refs[-1]
        rows = outs[0].shape[0]
        row, col = lax.axis_index("row"), lax.axis_index("col")
        for k, piece in enumerate(pieces):
            at = pl.multiple_of(place_of(col ^ k, row) * rows, rows)
            x_ref[pl.ds(at, rows), :] = piece[...]
    else:
        x_ref, *outs, token = refs
        rows = outs[0].shape[0]
    token[...] = jnp.zeros_like(token)

    def body(i):
        columns = pl.ds(pl.multiple_of(i * tile, tile), tile)
        load(i).wait()
        sums = jnp.dot(x_ref[...], buffer[:, columns], preferred_element_type=f32).astype(bf16)
        for k, out in enumerate(outs):
            out[:, columns] = sums[k * rows : (k + 1) * rows]

    each(size // tile, body)


def forward(x, weight, start, size, tokens, parts, dep=None):
    depth = weight.shape[0]
    tile = tile_of(size, TILE)
    rows = tokens // parts
    first = isinstance(x, tuple)
    operands = [weight, *x] if first else [weight, x]
    out_shape = [jax.ShapeDtypeStruct((rows, size), bf16)] * parts + [TOKEN]
    if first:
        out_shape.append(jax.ShapeDtypeStruct((tokens, depth), bf16))
    return call(
        functools.partial(forward_kernel, start, tile, parts, first),
        operands,
        [pl.BlockSpec(memory_space=pl.ANY)] + [resident()] * (len(operands) - 1),
        dep,
        out_specs=[resident()] * len(out_shape),
        out_shape=out_shape,
        scratch_shapes=[pltpu.VMEM((depth, size), bf16), pltpu.SemaphoreType.DMA((size // tile,))],
        compiler_params=params(36),
        cost_estimate=cost(2 * tokens * depth * size, 2 * depth * size),
        name="forward_sums",
    )


def stack_blocks(refs, all_ref):
    rows, width = refs[0].shape
    end = at_end()
    for q in range(len(refs) // 6):
        own, near, mid_m, mid_e, far_m, far_e = refs[6 * q : 6 * q + 6]
        columns = slice(q * width, (q + 1) * width)
        all_ref[0:rows, columns] = own[...]
        all_ref[rows : 2 * rows, columns] = near[...]

        @pl.when(jnp.logical_not(end))
        def _():
            all_ref[2 * rows : 3 * rows, columns] = mid_m[...]
            all_ref[3 * rows :, columns] = far_m[...]

        @pl.when(end)
        def _():
            all_ref[2 * rows : 3 * rows, columns] = mid_e[...]
            all_ref[3 * rows :, columns] = far_e[...]


def grads_kernel(names, start, lo, tile, *refs):
    ref = {}
    for name, one in zip(names, refs, strict=True):
        ref.setdefault(name, []).append(one)
    blocks, token = ref["block"], ref["token"][0]
    inputs, weight = "weight" in ref, "grad_weight" in ref
    delta = ref["delta"][0] if len(blocks) > 1 else blocks[0]
    size = delta.shape[1]
    tiles = (ref["loads"] if inputs else ref["stores"])[0].shape[0]
    hidden_copies = []
    if inputs:
        outs, before, w_tiles = ref["grad_inputs"], ref.get("before"), ref["weight_tiles"][0]
        load = functools.partial(
            fetch, ref["weight"][0], (lo, tiles * tile), (start, size), w_tiles, ref["loads"][0], tile, True
        )
        each(tiles, lambda i: load(i).start())
    for k, part in enumerate(ref.get("hidden", ())):
        columns = pl.ds(start + k * part.shape[1], part.shape[1])
        hidden_copies.append(
            pltpu.make_async_copy(part, ref["all_hidden"][0].at[:, columns], ref["hidden_sems"][0].at[k])
        )
        hidden_copies[-1].start()
    if len(blocks) > 1:
        stack_blocks(blocks, delta)
    token[...] = jnp.zeros_like(token)
    step = tile_of(size, 512)

    def store(i):
        at = pl.multiple_of(i * tile, tile)
        return pltpu.make_async_copy(
            ref["made_tiles"][0].at[pl.ds(at, tile), :],
            ref["grad_weight"][0].at[pl.ds(pl.multiple_of(lo + at, tile), tile), pl.ds(start, size)],
            ref["stores"][0].at[i],
        )

    def body(i):
        rows = pl.ds(pl.multiple_of(i * tile, tile), tile)
        if inputs:
            load(i).wait()
            value = lax.dot_general(
                delta[...], w_tiles[rows, :], (((1,), (1,)), ((), ())), preferred_element_type=f32
            )
            if before:
                value = value + before[0][:, rows]
            if len(outs) == 1:
                outs[0][:, rows] = value.astype(outs[0].dtype)
            else:
                staged = ref["staged"][0]
                staged[...] = value.astype(bf16)
                row, col = lax.axis_index("row"), lax.axis_index("col")
                tokens = outs[0].shape[0]
                for k, out in enumerate(outs):
                    at = pl.multiple_of(place_of(col ^ k, row) * tokens, tokens)
                    out[:, rows] = staged[pl.ds(at, tokens), :]
        if weight:
            x_t = ref["x"][0][:, pl.ds(pl.multiple_of(lo + i * tile, tile), tile)].T
            for at in range(0, size, step):
                ref["made_tiles"][0][rows, at : at + step] = jnp.dot(
                    x_t, delta[:, at : at + step], preferred_element_type=f32
                ).astype(bf16)
            store(i).start()

    if weight and UNROLL:
        for i in range(tiles):
            body(i)
    else:
        each(tiles, body)
    if weight:
        each(tiles, lambda i: store(i).wait())
    for copy in hidden_copies:
        copy.wait()


def grads(
    start, lo, hi, blocks, dep=None, *, weight=None, before=None, last=False, parts=1, x=None, into=None, hidden=(), all_hidden=None
):
    hbm = pl.BlockSpec(memory_space=pl.ANY)
    size = sum(b.shape[1] for b in blocks) if len(blocks) == 1 else blocks[0].shape[1] * (len(blocks) // 6)
    tokens = blocks[0].shape[0] * (4 if len(blocks) > 1 else 1)
    tile = tile_of(hi - lo, TILE)
    operands, outs, scratch, aliases = [], [], [], {}

    def give(name, value, spec=None):
        operands.append((name, value, spec or resident()))

    def make(name, shape, spec=None):
        outs.append((name, shape, spec or resident()))

    def carry(name, value):
        if not isinstance(value, jax.ShapeDtypeStruct):
            aliases[len(operands)] = len(outs)
            give(name + "_before", value, hbm)
        make(name, jax.ShapeDtypeStruct(value.shape, value.dtype), hbm)

    for block in blocks:
        give("block", block)
    if len(blocks) > 1:
        scratch.append(("delta", pltpu.VMEM((tokens, size), bf16)))
    tiles, sems = pltpu.VMEM((hi - lo, size), bf16), pltpu.SemaphoreType.DMA(((hi - lo) // tile,))
    if weight is not None:
        give("weight", weight, hbm)
        if before is not None:
            give("before", before)
        for _ in range(parts):
            make("grad_inputs", jax.ShapeDtypeStruct((tokens // parts, hi - lo), bf16 if last else f32))
        scratch += [("weight_tiles", tiles), ("loads", sems)]
        if parts > 1:
            scratch.append(("staged", pltpu.VMEM((tokens, tile), bf16)))
    if x is not None:
        give("x", x)
        carry("grad_weight", into)
        scratch += [("made_tiles", tiles), ("stores", sems)]
    if hidden:
        for part in hidden:
            give("hidden", part)
        carry("all_hidden", all_hidden)
        scratch.append(("hidden_sems", pltpu.SemaphoreType.DMA((len(hidden),))))
    make("token", TOKEN)
    names = [name for name, *_ in operands + outs + scratch]
    work = (weight is not None) + (x is not None)
    return call(
        functools.partial(grads_kernel, names, start, lo, tile),
        [value for _, value, _ in operands],
        [spec for *_, spec in operands],
        dep,
        out_specs=[spec for *_, spec in outs],
        out_shape=[shape for _, shape, _ in outs],
        scratch_shapes=[shape for _, shape in scratch],
        input_output_aliases=aliases,
        compiler_params=params(36),
        cost_estimate=cost(2 * work * tokens * (hi - lo) * size, 2 * work * (hi - lo) * size),
        name="grads",
    )


def call(kernel, operands, in_specs, dep, **options):
    count = len(operands)

    def ordered(*refs):
        kernel(*refs[:count], *refs[count + 1 :])

    if dep is None:
        return pl.pallas_call(kernel, in_specs=in_specs, **options)(*operands)
    in_specs = [*in_specs, pl.BlockSpec(memory_space=pl.ANY)]
    return pl.pallas_call(ordered, in_specs=in_specs, **options)(*operands, dep)


def combine(name, kernel, operands, outs, dep):
    vmem = pl.BlockSpec(memory_space=pltpu.VMEM)
    like = operands[0]
    moved = sum(o.size * 2 for o in operands)
    return call(
        kernel,
        operands,
        [vmem] * len(operands),
        dep,
        out_specs=[vmem] * outs,
        out_shape=[jax.ShapeDtypeStruct(like.shape, bf16)] * outs,
        compiler_params=params(16),
        cost_estimate=cost(moved, moved),
        name=name,
    )


def at_end():
    row = lax.axis_index("row")
    return (row == 0) | (row == 3)


def pick(out, at_ends, at_middles):
    end = at_end()

    @pl.when(end)
    def _():
        out[...] = at_ends[...]

    @pl.when(jnp.logical_not(end))
    def _():
        out[...] = at_middles[...]


def pass_on_kernel(a, out):
    out[...] = a[...]


def ends_in_kernel(far, mid_m, near_d, out, relay):
    pick(out, far, mid_m)
    relay[...] = near_d[...]


def copy_two_kernel(a, b, out_a, out_b):
    out_a[...] = a[...]
    out_b[...] = b[...]


def far_sum_kernel(mid, far_m, far, far_in, out, out_sum):
    pick(out, mid, far_m)
    out_sum[...] = far[...] + far_in[...]


def far_sum_only_kernel(mid, far, far_in, out, out_sum):
    out[...] = mid[...]
    out_sum[...] = far[...] + far_in[...]


def near_sum_kernel(near, far_sum, mid, mid_in, out, out_sum):
    end = at_end()
    out_sum[...] = mid[...] + mid_in[...]

    @pl.when(end)
    def _():
        out[...] = near[...]

    @pl.when(jnp.logical_not(end))
    def _():
        out[...] = near[...] + far_sum[...]


def gelu_kernel(own, near_sum, mid_sum, cotangent, hidden, delta):
    end = at_end()
    width = own.shape[1]
    step = 256 if width % 256 == 0 else width

    def body(j, carry):
        cols = pl.ds(pl.multiple_of(j * step, step), step)
        from_mid = jnp.where(end, 0.0, mid_sum[:, cols].astype(f32))
        preact = own[:, cols].astype(f32) + from_mid + near_sum[:, cols].astype(f32)
        value, slope = gelu_both(preact)
        hidden[:, cols] = value.astype(bf16)
        delta[:, cols] = (cotangent[:, cols].astype(f32) * slope).astype(bf16)
        return carry

    lax.fori_loop(0, width // step, body, 0)


def sum_kernel(a, b, out):
    out[...] = a[...] + b[...]


def finish_kernel(*refs):
    out = refs[-1]
    width = refs[0].shape[1]
    for k in range(SPLIT):
        keep, give, across = refs[3 * k : 3 * k + 3]
        out[:, k * width : (k + 1) * width] = (
            keep[...].astype(f32) + give[...].astype(f32) + across[...].astype(f32)
        ).astype(bf16)


def join(name, kernel, operands, shape, dep):
    moved = sum(o.size * 2 for o in operands)
    return call(
        kernel,
        list(operands),
        [resident()] * len(operands),
        dep,
        grid=(1,),
        out_specs=whole(*shape),
        out_shape=jax.ShapeDtypeStruct(shape, bf16),
        compiler_params=params(16),
        cost_estimate=cost(moved, moved),
        name=name,
    )


def gather_inputs(inputs):
    across = send(inputs, "col", ACROSS)
    (local,) = combine("local", pass_on_kernel, (inputs,), 1, None)
    beside = send(local, "col", CORES)
    corner = send(across, "col", CORES)
    return (local, beside, across, corner)


class Order:
    def __init__(self, plan):
        self.plan, self.steps, self.token = plan, 0, None

    def between(self, name, kernel, operands, outs=2):
        values = combine(name, kernel, operands, outs, self.token)
        self.token = values[0]
        return values

    def work(self):
        for kernel in self.plan.get(self.steps, ()):
            self.token = kernel(self.token)
        self.steps += 1


def on_line(inputs, weight, cotangent):
    depth, width = weight.shape
    tokens = 4 * inputs.shape[0]
    chunks = STREAMS * ROUNDS
    size = width // chunks
    cuts = [depth * k // SPLIT for k in range(SPLIT + 1)]
    bounds = list(zip(cuts[:-1], cuts[1:]))
    sums, delta, blocks, hidden = {}, {}, {}, {}
    total = [None] * SPLIT
    state = {
        "weight": jax.ShapeDtypeStruct(weight.shape, bf16),
        "hidden": jax.ShapeDtypeStruct(cotangent.shape, bf16),
    }
    plan = {}
    order = Order(plan)

    def forward_of(k):
        def run(dep):
            *sums[k], token = forward(x, weight, k * size, size, tokens, 4, dep)
            return token

        return run

    def grads_of(k, cut=SPLIT, part=0, both=True):
        def run(dep):
            mine = range(SPLIT) if cut == 1 else [part]
            more = {}
            if both:
                more = {"x": x, "into": state["weight"]}
                if part == 0:
                    more |= {"hidden": [hidden[k]], "all_hidden": state["hidden"]}
            lo, hi = bounds[mine[0]][0], bounds[mine[-1]][1]
            before = total[mine[0]]
            if before is not None and cut == 1:
                before = jnp.concatenate([total[p] for p in mine], axis=1)
            made = list(
                grads(k * size, lo, hi, blocks[k], dep, weight=weight, before=before, **more)
            )
            total[mine[0]] = made.pop(0)
            if both:
                state["weight"] = made.pop(0)
                if part == 0:
                    state["hidden"] = made.pop(0)
            return made.pop(0)

        return run

    def chain(mine):
        def exchange(values):
            return [send(value, PLANE, to) for value, to in zip(values, (HALVES, MIDDLE))]

        for at, k in enumerate([*mine, None]):
            before = mine[at - 1] if at else None
            if before is not None:
                own, near_sum, mid_sum = pending
                part = cotangent[:, before * size : (before + 1) * size]
                hidden[before], delta[before] = order.between(
                    "gelu", gelu_kernel, (own, near_sum, mid_sum, part)
                )
                near_d, mid_m = exchange((delta[before], delta[before]))
                order.work()
                yield
            if k is not None:
                own, near, mid, far = sums[k]
            if k is None:
                mid_e, far_m = exchange(order.between("relay", copy_two_kernel, (mid_m, near_d)))
                order.work()
                yield
                (far_e,) = exchange(order.between("relay_far", pass_on_kernel, (far_m,), 1))
            elif before is None:
                far_in = send(far, PLANE, HALVES)
                order.work()
                yield
                mid_in, far_sum = exchange(
                    order.between("far_sum", far_sum_only_kernel, (mid, far, far_in))
                )
            else:
                far_in, far_m = exchange(
                    order.between("ends_in", ends_in_kernel, (far, mid_m, near_d))
                )
                order.work()
                yield
                mid_in, far_sum = exchange(
                    order.between("far_sum", far_sum_kernel, (mid, far_m, far, far_in))
                )
                mid_e, far_e = far_in, mid_in
            if before is not None:
                blocks[before] = [delta[before], near_d, mid_m, mid_e, far_m, far_e]
            order.work()
            yield
            if k is not None:
                near_sum, mid_sum = exchange(
                    order.between("near_sum", near_sum_kernel, (near, far_sum, mid, mid_in))
                )
                pending = (own, near_sum, mid_sum)
                order.work()
                yield

    *sums[0], order.token, x = forward(gather_inputs(inputs), weight, 0, size, tokens, 4)
    plan.update(planned(forward_of, grads_of))
    chains = [chain(list(range(s, chunks, STREAMS))) for s in range(STREAMS)]
    live = list(chains)
    while live:
        for one in list(live):
            if next(one, live) is live:
                live.remove(one)

    final = chunks - 1
    for k in range(chunks - STREAMS, final):
        for part in range(SPLIT):
            order.token = grads_of(k, part=part, both=False)(order.token)
    parts, given = [], []
    for part, (lo, hi) in enumerate(bounds):
        *pieces, order.token = grads(
            final * size, lo, hi, blocks[final], order.token, weight=weight, before=total[part], last=True, parts=4
        )
        parts.append(pieces)
        given.append((send(pieces[3], "col", CORES), send(pieces[1], "col", CORES)))
    finals = []
    for (keep, _, keep_far, _), (far_in, near_in) in zip(parts, given):
        (far_sum,) = order.between("far_sum_col", sum_kernel, (keep_far, far_in), 1)
        finals += [keep, near_in, send(far_sum, "col", ACROSS)]
    late = range(chunks - STREAMS, chunks)
    grad_weight, all_hidden, order.token = grads(
        late[0] * size,
        0,
        depth,
        [block for k in late for block in blocks[k]],
        order.token,
        x=x,
        into=state["weight"],
        hidden=[hidden[k] for k in late],
        all_hidden=state["hidden"],
    )
    grad_inputs = join("finish", finish_kernel, finals, inputs.shape, order.token)
    return (all_hidden, grad_inputs, grad_weight)


def planned(forward_of, grads_of):
    return {
        0: [forward_of(1)],
        2: [forward_of(2)],
        4: [forward_of(3)],
        12: [grads_of(0, part=0)],
        14: [grads_of(0, part=1)],
        16: [grads_of(1, part=0)],
        18: [grads_of(1, part=1)],
    }


def on_any(inputs, weight, cotangent):
    depth, width = weight.shape
    x = lax.all_gather(inputs, "col", axis=0, tiled=True)
    tokens = x.shape[0]
    sums, _ = forward(x, weight, 0, width, tokens, 1)
    preact = lax.psum_scatter(sums, "row", scatter_dimension=0, tiled=True).astype(f32)
    value, slope = gelu_both(preact)
    delta = (cotangent.astype(f32) * slope).astype(bf16)
    blocks = [lax.all_gather(delta, "row", axis=0, tiled=True)]
    made = jax.ShapeDtypeStruct(weight.shape, bf16)
    sums, grad_weight, _ = grads(0, 0, depth, blocks, weight=weight, last=True, x=x, into=made)
    grad_inputs = lax.psum_scatter(sums, "col", scatter_dimension=0, tiled=True)
    return (value.astype(bf16), grad_inputs, grad_weight)


def solution(mesh):
    in_specs = (P(("groups", "col"), "row"), P("row", "col"), P(("groups", "row"), "col"))
    out_specs = (
        P(("groups", "row"), "col"),
        P(("groups", "col"), "row"),
        P(("groups", "row"), "col"),
    )
    fits = mesh.shape["row"] == 4 and mesh.shape["col"] == 4
    return jax.shard_map(
        on_line if fits else on_any,
        mesh=mesh,
        in_specs=in_specs,
        out_specs=out_specs,
        check_vma=False,
    )
```

```python
import functools

import jax
import jax.numpy as jnp
from jax import lax
from jax.experimental import pallas as pl
from jax.experimental.pallas import tpu as pltpu
from jax.sharding import PartitionSpec as P

tanh_scale = 0.7978845608028654
cubic_coef = 0.044715
bf16 = jnp.bfloat16
f32 = jnp.float32
MIB = 1 << 20

CORES = ((0, 1), (1, 0), (2, 3), (3, 2))
ACROSS = ((0, 2), (2, 0), (1, 3), (3, 1))
PLANE = ("row", "col")
HALVES = tuple((4 * row + col, 4 * (row ^ 1) + col) for row in range(4) for col in range(4))
MIDDLE = tuple(
    (4 * row + col, 4 * (3 - row) + col if row in (1, 2) else 4 * row + (col ^ 1))
    for row in range(4)
    for col in range(4)
)

STREAMS = 2
ROUNDS = 2
SPLIT = 2
EARLY = 2


def gelu_both(preact):
    inner = tanh_scale * (preact + cubic_coef * preact * preact * preact)
    tangent = jnp.tanh(inner)
    value = 0.5 * preact * (1.0 + tangent)
    slope = 0.5 * (1.0 + tangent) + 0.5 * preact * (1.0 - tangent * tangent) * tanh_scale * (
        1.0 + 3.0 * cubic_coef * preact * preact
    )
    return value, slope


def send(value, axis, pairs):
    return lax.ppermute(value, axis, pairs)


def place_of(token_block, row):
    same_half = (token_block // 2) == (row // 2)
    return jnp.where(same_half, token_block ^ row, jnp.where(row < 2, token_block, 3 - token_block))


def params(limit=48):
    return pltpu.CompilerParams(vmem_limit_bytes=limit * MIB)


def cost(flops, bytes_accessed):
    return pl.CostEstimate(flops=int(flops), bytes_accessed=int(bytes_accessed), transcendentals=0)


def whole(*shape):
    return pl.BlockSpec(shape, lambda j: (0,) * len(shape))


def resident():
    return pl.BlockSpec(memory_space=pltpu.VMEM)


def tile_of(size, want):
    tile = want
    while size % tile:
        tile //= 2
    return tile


TILE = 512
UNROLL = True
TOKEN = jax.ShapeDtypeStruct((8, 128), f32)


def fetch(source, rows, columns, buffer, sems, tile, by_rows, i):
    at = pl.ds(pl.multiple_of(i * tile, tile), tile)
    if by_rows:
        part = source.at[pl.ds(pl.multiple_of(rows[0] + i * tile, tile), tile), pl.ds(*columns)]
        return pltpu.make_async_copy(part, buffer.at[at, :], sems.at[i])
    part = source.at[pl.ds(*rows), pl.ds(pl.multiple_of(columns[0] + i * tile, tile), tile)]
    return pltpu.make_async_copy(part, buffer.at[:, at], sems.at[i])


def each(count, body):
    def run(i, carry):
        body(i)
        return carry

    lax.fori_loop(0, count, run, 0)


def preload_kernel(starts, w_ref, *refs):
    *outs, sems = refs
    copies = []
    for k, (start, out) in enumerate(zip(starts, outs)):
        part = w_ref.at[:, pl.ds(start, out.shape[1])]
        copies.append(pltpu.make_async_copy(part, out, sems.at[k]))
        copies[-1].start()
    for copy in copies:
        copy.wait()


def preload(weight, starts, size, dep):
    shape = jax.ShapeDtypeStruct((weight.shape[0], size), bf16)
    return call(
        functools.partial(preload_kernel, starts),
        [weight],
        [pl.BlockSpec(memory_space=pl.ANY)],
        dep,
        out_specs=[resident()] * len(starts),
        out_shape=[shape] * len(starts),
        scratch_shapes=[pltpu.SemaphoreType.DMA((len(starts),))],
        compiler_params=params(16),
        cost_estimate=cost(0, 2 * len(starts) * shape.size),
        name="preload",
    )


def forward_kernel(start, tile, parts, first, loaded, w_ref, *refs):
    if loaded:
        buffer = w_ref
    else:
        *refs, buffer, sems = refs
    depth, size = buffer.shape
    if not loaded:
        load = functools.partial(fetch, w_ref, (0, depth), (start, size), buffer, sems, tile, False)
        each(size // tile, lambda i: load(i).start())
    if first:
        pieces, outs, token, x_ref = refs[:parts], refs[parts : 2 * parts], refs[-2], refs[-1]
        rows = outs[0].shape[0]
        row, col = lax.axis_index("row"), lax.axis_index("col")
        for k, piece in enumerate(pieces):
            at = pl.multiple_of(place_of(col ^ k, row) * rows, rows)
            x_ref[pl.ds(at, rows), :] = piece[...]
    else:
        x_ref, *outs, token = refs
        rows = outs[0].shape[0]
    token[...] = jnp.zeros_like(token)

    def body(i):
        columns = pl.ds(pl.multiple_of(i * tile, tile), tile)
        if not loaded:
            load(i).wait()
        sums = jnp.dot(x_ref[...], buffer[:, columns], preferred_element_type=f32).astype(bf16)
        for k, out in enumerate(outs):
            out[:, columns] = sums[k * rows : (k + 1) * rows]

    each(size // tile, body)


def forward(x, weight, start, size, tokens, parts, dep=None, loaded=None):
    depth = weight.shape[0]
    tile = tile_of(size, TILE)
    rows = tokens // parts
    first = isinstance(x, tuple)
    here = loaded is not None
    operands = [loaded if here else weight, *(x if first else (x,))]
    out_shape = [jax.ShapeDtypeStruct((rows, size), bf16)] * parts + [TOKEN]
    if first:
        out_shape.append(jax.ShapeDtypeStruct((tokens, depth), bf16))
    scratch = [pltpu.VMEM((depth, size), bf16), pltpu.SemaphoreType.DMA((size // tile,))]
    return call(
        functools.partial(forward_kernel, start, tile, parts, first, here),
        operands,
        [resident() if here else pl.BlockSpec(memory_space=pl.ANY)] + [resident()] * (len(operands) - 1),
        dep,
        out_specs=[resident()] * len(out_shape),
        out_shape=out_shape,
        scratch_shapes=[] if here else scratch,
        compiler_params=params(16 if here else 36),
        cost_estimate=cost(2 * tokens * depth * size, 2 * depth * size),
        name="forward_sums",
    )


def stack_blocks(refs, all_ref):
    rows, width = refs[0].shape
    end = at_end()
    for q in range(len(refs) // 6):
        own, near, mid_m, mid_e, far_m, far_e = refs[6 * q : 6 * q + 6]
        columns = slice(q * width, (q + 1) * width)
        all_ref[0:rows, columns] = own[...]
        all_ref[rows : 2 * rows, columns] = near[...]

        @pl.when(jnp.logical_not(end))
        def _():
            all_ref[2 * rows : 3 * rows, columns] = mid_m[...]
            all_ref[3 * rows :, columns] = far_m[...]

        @pl.when(end)
        def _():
            all_ref[2 * rows : 3 * rows, columns] = mid_e[...]
            all_ref[3 * rows :, columns] = far_e[...]


def grads_kernel(names, start, cuts, tile, *refs):
    ref = {}
    for name, one in zip(names, refs, strict=True):
        ref.setdefault(name, []).append(one)
    blocks, token = ref["block"], ref["token"][0]
    inputs, weight = "weight" in ref or "loaded" in ref, "grad_weight" in ref
    loaded = "loaded" in ref
    delta = ref["delta"][0] if len(blocks) > 1 else blocks[0]
    size = delta.shape[1]
    lo, tiles = cuts[0][0], (cuts[-1][1] - cuts[0][0]) // tile
    w_first = lo if loaded else 0
    hidden_copies = []
    if inputs:
        outs, before = ref["grad_inputs"], ref.get("before")
        w_tiles = (ref["loaded"] if loaded else ref["weight_tiles"])[0]
        parts = len(outs) // len(cuts)
    if inputs and not loaded:
        load = functools.partial(
            fetch, ref["weight"][0], (lo, tiles * tile), (start, size), w_tiles, ref["loads"][0], tile, True
        )
        each(tiles, lambda i: load(i).start())
    for k, part in enumerate(ref.get("hidden", ())):
        columns = pl.ds(start + k * part.shape[1], part.shape[1])
        hidden_copies.append(
            pltpu.make_async_copy(part, ref["all_hidden"][0].at[:, columns], ref["hidden_sems"][0].at[k])
        )
        hidden_copies[-1].start()
    if len(blocks) > 1:
        stack_blocks(blocks, delta)
    token[...] = jnp.zeros_like(token)
    step = tile_of(size, 512)

    def store(i):
        at = pl.multiple_of(i * tile, tile)
        return pltpu.make_async_copy(
            ref["made_tiles"][0].at[pl.ds(at, tile), :],
            ref["grad_weight"][0].at[pl.ds(pl.multiple_of(lo + at, tile), tile), pl.ds(start, size)],
            ref["stores"][0].at[i],
        )

    def body(cut, first, i):
        rows = pl.ds(pl.multiple_of(i * tile, tile), tile)
        if weight:
            x_t = ref["x"][0][:, pl.ds(pl.multiple_of(lo + i * tile, tile), tile)].T
            for at in range(0, size, step):
                ref["made_tiles"][0][rows, at : at + step] = jnp.dot(
                    x_t, delta[:, at : at + step], preferred_element_type=f32
                ).astype(bf16)
            store(i).start()
        if inputs:
            if not loaded:
                load(i).wait()
            w_rows = pl.ds(pl.multiple_of(w_first + i * tile, tile), tile)
            value = lax.dot_general(
                delta[...], w_tiles[w_rows, :], (((1,), (1,)), ((), ())), preferred_element_type=f32
            )
            into = pl.ds(pl.multiple_of((i - first) * tile, tile), tile)
            if before:
                value = value + before[cut][:, into]
            if parts == 1:
                outs[cut][:, into] = value.astype(outs[cut].dtype)
            else:
                staged = ref["staged"][0]
                staged[...] = value.astype(bf16)
                row, col = lax.axis_index("row"), lax.axis_index("col")
                tokens = outs[0].shape[0]
                for k in range(parts):
                    at = pl.multiple_of(place_of(col ^ k, row) * tokens, tokens)
                    outs[cut * parts + k][:, into] = staged[pl.ds(at, tokens), :]

    for cut, (low, high) in enumerate(cuts):
        first, past = (low - lo) // tile, (high - lo) // tile
        if weight and UNROLL:
            for i in range(first, past):
                body(cut, first, i)
        else:
            each(past - first, lambda i: body(cut, first, first + i))
    if weight:
        each(tiles, lambda i: store(i).wait())
    for copy in hidden_copies:
        copy.wait()


def grads(
    start, cuts, blocks, dep=None, *, weight=None, loaded=None, before=None, last=False, parts=1, x=None, into=None, hidden=(), all_hidden=None
):
    hbm = pl.BlockSpec(memory_space=pl.ANY)
    size = sum(b.shape[1] for b in blocks) if len(blocks) == 1 else blocks[0].shape[1] * (len(blocks) // 6)
    tokens = blocks[0].shape[0] * (4 if len(blocks) > 1 else 1)
    features = cuts[-1][1] - cuts[0][0]
    tile = tile_of(cuts[0][1] - cuts[0][0], TILE)
    operands, outs, scratch, aliases = [], [], [], {}

    def give(name, value, spec=None):
        operands.append((name, value, spec or resident()))

    def make(name, shape, spec=None):
        outs.append((name, shape, spec or resident()))

    def carry(name, value):
        if not isinstance(value, jax.ShapeDtypeStruct):
            aliases[len(operands)] = len(outs)
            give(name + "_before", value, hbm)
        make(name, jax.ShapeDtypeStruct(value.shape, value.dtype), hbm)

    for block in blocks:
        give("block", block)
    if len(blocks) > 1:
        scratch.append(("delta", pltpu.VMEM((tokens, size), bf16)))
    tiles, sems = pltpu.VMEM((features, size), bf16), pltpu.SemaphoreType.DMA((features // tile,))
    if weight is not None or loaded is not None:
        if loaded is None:
            give("weight", weight, hbm)
            scratch += [("weight_tiles", tiles), ("loads", sems)]
        else:
            give("loaded", loaded)
        for one in before or ():
            give("before", one)
        for low, high in cuts:
            shape = jax.ShapeDtypeStruct((tokens // parts, high - low), bf16 if last else f32)
            for _ in range(parts):
                make("grad_inputs", shape)
        if parts > 1:
            scratch.append(("staged", pltpu.VMEM((tokens, tile), bf16)))
    if x is not None:
        give("x", x)
        carry("grad_weight", into)
        scratch += [("made_tiles", tiles), ("stores", sems)]
    if hidden:
        for part in hidden:
            give("hidden", part)
        carry("all_hidden", all_hidden)
        scratch.append(("hidden_sems", pltpu.SemaphoreType.DMA((len(hidden),))))
    make("token", TOKEN)
    names = [name for name, *_ in operands + outs + scratch]
    work = (weight is not None or loaded is not None) + (x is not None)
    return call(
        functools.partial(grads_kernel, names, start, cuts, tile),
        [value for _, value, _ in operands],
        [spec for *_, spec in operands],
        dep,
        out_specs=[spec for *_, spec in outs],
        out_shape=[shape for _, shape, _ in outs],
        scratch_shapes=[shape for _, shape in scratch],
        input_output_aliases=aliases,
        compiler_params=params(36),
        cost_estimate=cost(2 * work * tokens * features * size, 2 * work * features * size),
        name="grads",
    )


def call(kernel, operands, in_specs, dep, **options):
    count = len(operands)

    def ordered(*refs):
        kernel(*refs[:count], *refs[count + 1 :])

    if dep is None:
        return pl.pallas_call(kernel, in_specs=in_specs, **options)(*operands)
    in_specs = [*in_specs, pl.BlockSpec(memory_space=pl.ANY)]
    return pl.pallas_call(ordered, in_specs=in_specs, **options)(*operands, dep)


def combine(name, kernel, operands, outs, dep):
    vmem = pl.BlockSpec(memory_space=pltpu.VMEM)
    like = operands[0]
    moved = sum(o.size * 2 for o in operands)
    return call(
        kernel,
        operands,
        [vmem] * len(operands),
        dep,
        out_specs=[vmem] * outs,
        out_shape=[jax.ShapeDtypeStruct(like.shape, bf16)] * outs,
        compiler_params=params(16),
        cost_estimate=cost(moved, moved),
        name=name,
    )


def at_end():
    row = lax.axis_index("row")
    return (row == 0) | (row == 3)


def pick(out, at_ends, at_middles):
    end = at_end()

    @pl.when(end)
    def _():
        out[...] = at_ends[...]

    @pl.when(jnp.logical_not(end))
    def _():
        out[...] = at_middles[...]


def pass_on_kernel(a, out):
    out[...] = a[...]


def ends_in_kernel(far, mid_m, near_d, out, relay):
    pick(out, far, mid_m)
    relay[...] = near_d[...]


def copy_two_kernel(a, b, out_a, out_b):
    out_a[...] = a[...]
    out_b[...] = b[...]


def far_sum_kernel(mid, far_m, far, far_in, out, out_sum):
    pick(out, mid, far_m)
    out_sum[...] = far[...] + far_in[...]


def far_sum_only_kernel(mid, far, far_in, out, out_sum):
    out[...] = mid[...]
    out_sum[...] = far[...] + far_in[...]


def near_sum_kernel(near, far_sum, mid, mid_in, out, out_sum):
    end = at_end()
    out_sum[...] = mid[...] + mid_in[...]

    @pl.when(end)
    def _():
        out[...] = near[...]

    @pl.when(jnp.logical_not(end))
    def _():
        out[...] = near[...] + far_sum[...]


def gelu_kernel(own, near_sum, mid_sum, cotangent, hidden, delta):
    end = at_end()
    width = own.shape[1]
    step = 256 if width % 256 == 0 else width

    def body(j, carry):
        cols = pl.ds(pl.multiple_of(j * step, step), step)
        from_mid = jnp.where(end, 0.0, mid_sum[:, cols].astype(f32))
        preact = own[:, cols].astype(f32) + from_mid + near_sum[:, cols].astype(f32)
        value, slope = gelu_both(preact)
        hidden[:, cols] = value.astype(bf16)
        delta[:, cols] = (cotangent[:, cols].astype(f32) * slope).astype(bf16)
        return carry

    lax.fori_loop(0, width // step, body, 0)


def sum_kernel(a, b, c, out, relay):
    out[...] = a[...] + b[...]
    relay[...] = c[...]


def finish_kernel(*refs):
    out = refs[-1]
    width = refs[0].shape[1]
    for k in range(SPLIT):
        keep, give, across = refs[3 * k : 3 * k + 3]
        out[:, k * width : (k + 1) * width] = (
            keep[...].astype(f32) + give[...].astype(f32) + across[...].astype(f32)
        ).astype(bf16)


def join(name, kernel, operands, shape, dep):
    moved = sum(o.size * 2 for o in operands)
    return call(
        kernel,
        list(operands),
        [resident()] * len(operands),
        dep,
        grid=(1,),
        out_specs=whole(*shape),
        out_shape=jax.ShapeDtypeStruct(shape, bf16),
        compiler_params=params(16),
        cost_estimate=cost(moved, moved),
        name=name,
    )


def gather_inputs(inputs, meanwhile):
    across = send(inputs, "col", ACROSS)
    (local,) = combine("local", pass_on_kernel, (inputs,), 1, None)
    beside = send(local, "col", CORES)
    made = meanwhile(local)
    (relayed,) = combine("corner", pass_on_kernel, (across,), 1, made[0])
    corner = send(relayed, "col", CORES)
    return (local, beside, relayed, corner), made


class Order:
    def __init__(self, plan):
        self.plan, self.steps, self.token = plan, 0, None

    def between(self, name, kernel, operands, outs=2):
        values = combine(name, kernel, operands, outs, self.token)
        self.token = values[0]
        return values

    def work(self):
        for kernel in self.plan.get(self.steps, ()):
            self.token = kernel(self.token)
        self.steps += 1


def on_line(inputs, weight, cotangent):
    depth, width = weight.shape
    tokens = 4 * inputs.shape[0]
    chunks = STREAMS * ROUNDS
    size = width // chunks
    cuts = [depth * k // SPLIT for k in range(SPLIT + 1)]
    bounds = list(zip(cuts[:-1], cuts[1:]))
    sums, delta, blocks, hidden = {}, {}, {}, {}
    total = [None] * SPLIT
    state = {
        "weight": jax.ShapeDtypeStruct(weight.shape, bf16),
        "hidden": jax.ShapeDtypeStruct(cotangent.shape, bf16),
    }
    plan = {}
    order = Order(plan)

    def forward_of(k):
        def run(dep):
            *sums[k], token = forward(x, weight, k * size, size, tokens, 4, dep, loaded.get(k))
            return token

        return run

    def grads_of(k, *which, both=True):
        def run(dep):
            more = {}
            if both:
                more = {"x": x, "into": state["weight"]}
                if which[0] == 0:
                    more |= {"hidden": [hidden[k]], "all_hidden": state["hidden"]}
            before = [total[p] for p in which] if total[which[0]] is not None else None
            made = list(
                grads(k * size, [bounds[p] for p in which], blocks[k], dep, weight=weight, before=before, **more)
            )
            for p in which:
                total[p] = made.pop(0)
            if both:
                state["weight"] = made.pop(0)
                if which[0] == 0:
                    state["hidden"] = made.pop(0)
            return made.pop(0)

        return run

    def preload_of(k):
        def run(dep):
            (loaded[k],) = preload(weight, [k * size], size, dep)
            return loaded[k]

        return run

    def chain(mine):
        def exchange(values):
            return [send(value, PLANE, to) for value, to in zip(values, (HALVES, MIDDLE))]

        for at, k in enumerate([*mine, None]):
            before = mine[at - 1] if at else None
            if before is not None:
                own, near_sum, mid_sum = pending
                part = cotangent[:, before * size : (before + 1) * size]
                hidden[before], delta[before] = order.between(
                    "gelu", gelu_kernel, (own, near_sum, mid_sum, part)
                )
                near_d, mid_m = exchange((delta[before], delta[before]))
                order.work()
                yield
            if k is not None:
                own, near, mid, far = sums[k]
            if k is None:
                mid_e, far_m = exchange(order.between("relay", copy_two_kernel, (mid_m, near_d)))
                order.work()
                yield
                (far_e,) = exchange(order.between("relay_far", pass_on_kernel, (far_m,), 1))
            elif before is None:
                far_in = send(far, PLANE, HALVES)
                order.work()
                yield
                mid_in, far_sum = exchange(
                    order.between("far_sum", far_sum_only_kernel, (mid, far, far_in))
                )
            else:
                far_in, far_m = exchange(
                    order.between("ends_in", ends_in_kernel, (far, mid_m, near_d))
                )
                order.work()
                yield
                mid_in, far_sum = exchange(
                    order.between("far_sum", far_sum_kernel, (mid, far_m, far, far_in))
                )
                mid_e, far_e = far_in, mid_in
            if before is not None:
                blocks[before] = [delta[before], near_d, mid_m, mid_e, far_m, far_e]
            order.work()
            yield
            if k is not None:
                near_sum, mid_sum = exchange(
                    order.between("near_sum", near_sum_kernel, (near, far_sum, mid, mid_in))
                )
                pending = (own, near_sum, mid_sum)
                order.work()
                yield

    early = range(EARLY)
    pieces, made = gather_inputs(
        inputs, lambda dep: preload(weight, [k * size for k in early], size, dep)
    )
    loaded = dict(zip(early, made))
    *sums[0], order.token, x = forward(pieces, weight, 0, size, tokens, 4, None, loaded.get(0))
    plan.update(planned(forward_of, grads_of, preload_of))
    chains = [chain(list(range(s, chunks, STREAMS))) for s in range(STREAMS)]
    live = list(chains)
    while live:
        for one in list(live):
            if next(one, live) is live:
                live.remove(one)

    final = chunks - 1
    for k in range(chunks - STREAMS, final):
        order.token = grads_of(k, *range(SPLIT), both=False)(order.token)
    finals, parts, far_in = [], [], []

    def across(part):
        keep, give, keep_far, _ = parts[part]
        far_sum, give = order.between("far_sum_col", sum_kernel, (keep_far, far_in[part], give))
        finals.extend([keep, send(far_sum, "col", ACROSS), send(give, "col", CORES)])

    for part, cut in enumerate(bounds):
        *pieces, order.token = grads(
            final * size,
            [cut],
            blocks[final],
            order.token,
            weight=weight,
            loaded=loaded.get(final),
            before=[total[part]],
            last=True,
            parts=4,
        )
        if part:
            across(part - 1)
        parts.append(pieces)
        far_in.append(send(pieces[3], "col", CORES))
    across(SPLIT - 1)
    late = range(chunks - STREAMS, chunks)
    grad_weight, all_hidden, order.token = grads(
        late[0] * size,
        [(0, depth)],
        [block for k in late for block in blocks[k]],
        order.token,
        x=x,
        into=state["weight"],
        hidden=[hidden[k] for k in late],
        all_hidden=state["hidden"],
    )
    grad_inputs = join("finish", finish_kernel, finals, inputs.shape, order.token)
    return (all_hidden, grad_inputs, grad_weight)


def planned(forward_of, grads_of, preload_of):
    return {
        0: [forward_of(1)],
        2: [forward_of(2)],
        4: [forward_of(3)],
        12: [grads_of(0, 0)],
        14: [grads_of(0, 1)],
        16: [grads_of(1, 0)],
        18: [grads_of(1, 1)],
        19: [preload_of(3)],
    }


def on_any(inputs, weight, cotangent):
    depth, width = weight.shape
    x = lax.all_gather(inputs, "col", axis=0, tiled=True)
    tokens = x.shape[0]
    sums, _ = forward(x, weight, 0, width, tokens, 1)
    preact = lax.psum_scatter(sums, "row", scatter_dimension=0, tiled=True).astype(f32)
    value, slope = gelu_both(preact)
    delta = (cotangent.astype(f32) * slope).astype(bf16)
    blocks = [lax.all_gather(delta, "row", axis=0, tiled=True)]
    made = jax.ShapeDtypeStruct(weight.shape, bf16)
    sums, grad_weight, _ = grads(0, [(0, depth)], blocks, weight=weight, last=True, x=x, into=made)
    grad_inputs = lax.psum_scatter(sums, "col", scatter_dimension=0, tiled=True)
    return (value.astype(bf16), grad_inputs, grad_weight)


def solution(mesh):
    in_specs = (P(("groups", "col"), "row"), P("row", "col"), P(("groups", "row"), "col"))
    out_specs = (
        P(("groups", "row"), "col"),
        P(("groups", "col"), "row"),
        P(("groups", "row"), "col"),
    )
    fits = mesh.shape["row"] == 4 and mesh.shape["col"] == 4
    return jax.shard_map(
        on_line if fits else on_any,
        mesh=mesh,
        in_specs=in_specs,
        out_specs=out_specs,
        check_vma=False,
    )
```

```python
import functools
import math

import jax
import jax.numpy as jnp
from jax import lax
from jax.experimental import pallas as pl
from jax.experimental.pallas import tpu as pltpu
from jax.sharding import PartitionSpec as P

tanh_scale = 0.7978845608028654
cubic_coef = 0.044715
bf16 = jnp.bfloat16
f32 = jnp.float32
MIB = 1 << 20

CORES = ((0, 1), (1, 0), (2, 3), (3, 2))
ACROSS = ((0, 2), (2, 0), (1, 3), (3, 1))
PLANE = ("row", "col")
HALVES = tuple((4 * row + col, 4 * (row ^ 1) + col) for row in range(4) for col in range(4))
MIDDLE = tuple(
    (4 * row + col, 4 * (3 - row) + col if row in (1, 2) else 4 * row + (col ^ 1))
    for row in range(4)
    for col in range(4)
)

STREAMS = 2
ROUNDS = 2
SPLIT = 2
EARLY = 2


def gelu_both(preact):
    inner = tanh_scale * (preact + cubic_coef * preact * preact * preact)
    tangent = jnp.tanh(inner)
    value = 0.5 * preact * (1.0 + tangent)
    slope = 0.5 * (1.0 + tangent) + 0.5 * preact * (1.0 - tangent * tangent) * tanh_scale * (
        1.0 + 3.0 * cubic_coef * preact * preact
    )
    return value, slope


def send(value, axis, pairs):
    return lax.ppermute(value, axis, pairs)


def place_of(token_block, row):
    same_half = (token_block // 2) == (row // 2)
    return jnp.where(same_half, token_block ^ row, jnp.where(row < 2, token_block, 3 - token_block))


def params(limit=48):
    return pltpu.CompilerParams(vmem_limit_bytes=limit * MIB)


def cost(flops, bytes_accessed):
    return pl.CostEstimate(flops=int(flops), bytes_accessed=int(bytes_accessed), transcendentals=0)


def whole(*shape):
    return pl.BlockSpec(shape, lambda j: (0,) * len(shape))


def resident():
    return pl.BlockSpec(memory_space=pltpu.VMEM)


def tile_of(size, want):
    tile = want
    while size % tile:
        tile //= 2
    return tile


TILE = 512
EXTRA = 4
UNROLL = True
TOKEN = jax.ShapeDtypeStruct((8, 128), f32)


def fetch(source, rows, columns, buffer, sems, tile, by_rows, i):
    at = pl.ds(pl.multiple_of(i * tile, tile), tile)
    if by_rows:
        part = source.at[pl.ds(pl.multiple_of(rows[0] + i * tile, tile), tile), pl.ds(*columns)]
        return pltpu.make_async_copy(part, buffer.at[at, :], sems.at[i])
    part = source.at[pl.ds(*rows), pl.ds(pl.multiple_of(columns[0] + i * tile, tile), tile)]
    return pltpu.make_async_copy(part, buffer.at[:, at], sems.at[i])


def each(count, body):
    def run(i, carry):
        body(i)
        return carry

    lax.fori_loop(0, count, run, 0)


def preload_kernel(starts, w_ref, *refs):
    *outs, sems = refs
    copies = []
    for k, (start, out) in enumerate(zip(starts, outs)):
        part = w_ref.at[:, pl.ds(start, out.shape[1])]
        copies.append(pltpu.make_async_copy(part, out, sems.at[k]))
        copies[-1].start()
    for copy in copies:
        copy.wait()


def preload(weight, starts, size, dep):
    shape = jax.ShapeDtypeStruct((weight.shape[0], size), bf16)
    return call(
        functools.partial(preload_kernel, starts),
        [weight],
        [pl.BlockSpec(memory_space=pl.ANY)],
        dep,
        out_specs=[resident()] * len(starts),
        out_shape=[shape] * len(starts),
        scratch_shapes=[pltpu.SemaphoreType.DMA((len(starts),))],
        compiler_params=params(16),
        cost_estimate=cost(0, 2 * len(starts) * shape.size),
        name="preload",
    )


def forward_kernel(start, tile, parts, first, loaded, following, w_ref, *refs):
    ahead = None
    if following is not None:
        source, *refs, made, sem = refs
        ahead = pltpu.make_async_copy(
            source.at[:, pl.ds(following, made.shape[1])], made, sem.at[0]
        )
        ahead.start()
    if loaded:
        buffer = w_ref
    else:
        *refs, buffer, sems = refs
    depth, size = buffer.shape
    if not loaded:
        load = functools.partial(fetch, w_ref, (0, depth), (start, size), buffer, sems, tile, False)
        each(size // tile, lambda i: load(i).start())
    if first:
        pieces, outs, token, x_ref = refs[:parts], refs[parts : 2 * parts], refs[-2], refs[-1]
        rows = outs[0].shape[0]
        row, col = lax.axis_index("row"), lax.axis_index("col")
        for k, piece in enumerate(pieces):
            at = pl.multiple_of(place_of(col ^ k, row) * rows, rows)
            x_ref[pl.ds(at, rows), :] = piece[...]
    else:
        x_ref, *outs, token = refs
        rows = outs[0].shape[0]
    token[...] = jnp.zeros_like(token)

    def body(i):
        columns = pl.ds(pl.multiple_of(i * tile, tile), tile)
        if not loaded:
            load(i).wait()
        sums = jnp.dot(x_ref[...], buffer[:, columns], preferred_element_type=f32).astype(bf16)
        for k, out in enumerate(outs):
            out[:, columns] = sums[k * rows : (k + 1) * rows]

    each(size // tile, body)
    if ahead is not None:
        ahead.wait()


def forward(x, weight, start, size, tokens, parts, dep=None, loaded=None, following=None):
    depth = weight.shape[0]
    tile = tile_of(size, TILE)
    rows = tokens // parts
    first = isinstance(x, tuple)
    here = loaded is not None
    operands = [loaded if here else weight, *(x if first else (x,))]
    specs = [resident() if here else pl.BlockSpec(memory_space=pl.ANY)] + [resident()] * (len(operands) - 1)
    if following is not None:
        operands.insert(1, weight)
        specs.insert(1, pl.BlockSpec(memory_space=pl.ANY))
    out_shape = [jax.ShapeDtypeStruct((rows, size), bf16)] * parts + [TOKEN]
    if first:
        out_shape.append(jax.ShapeDtypeStruct((tokens, depth), bf16))
    scratch = [] if here else [pltpu.VMEM((depth, size), bf16), pltpu.SemaphoreType.DMA((size // tile,))]
    if following is not None:
        assert here and not first
        out_shape.append(jax.ShapeDtypeStruct((depth, size), bf16))
        scratch.append(pltpu.SemaphoreType.DMA((1,)))
    return call(
        functools.partial(forward_kernel, start, tile, parts, first, here, following),
        operands,
        specs,
        dep,
        out_specs=[resident()] * len(out_shape),
        out_shape=out_shape,
        scratch_shapes=scratch,
        compiler_params=params(12 if here else 36),
        cost_estimate=cost(2 * tokens * depth * size, 2 * depth * size),
        name="forward_sums",
    )


def stack_blocks(refs, all_ref):
    rows, width = refs[0].shape
    end = at_end()
    for q in range(len(refs) // 6):
        own, near, mid_m, mid_e, far_m, far_e = refs[6 * q : 6 * q + 6]
        columns = slice(q * width, (q + 1) * width)
        all_ref[0:rows, columns] = own[...]
        all_ref[rows : 2 * rows, columns] = near[...]

        @pl.when(jnp.logical_not(end))
        def _():
            all_ref[2 * rows : 3 * rows, columns] = mid_m[...]
            all_ref[3 * rows :, columns] = far_m[...]

        @pl.when(end)
        def _():
            all_ref[2 * rows : 3 * rows, columns] = mid_e[...]
            all_ref[3 * rows :, columns] = far_e[...]


def grads_kernel(names, start, cuts, tile, *refs):
    ref = {}
    for name, one in zip(names, refs, strict=True):
        ref.setdefault(name, []).append(one)
    blocks, token = ref["block"], ref["token"][0]
    inputs, weight = "weight" in ref or "loaded" in ref, "grad_weight" in ref
    loaded = "loaded" in ref
    delta = ref["delta"][0] if len(blocks) > 1 else blocks[0]
    size = delta.shape[1]
    lo, tiles = cuts[0][0], (cuts[-1][1] - cuts[0][0]) // tile
    w_first = lo if loaded else 0
    hidden_copies = []
    if inputs:
        outs, before = ref["grad_inputs"], ref.get("before")
        w_tiles = (ref["loaded"] if loaded else ref["weight_tiles"])[0]
        parts = len(outs) // len(cuts)
    if inputs and not loaded:
        load = functools.partial(
            fetch, ref["weight"][0], (lo, tiles * tile), (start, size), w_tiles, ref["loads"][0], tile, True
        )
        each(tiles, lambda i: load(i).start())
    for k, part in enumerate(ref.get("hidden", ())):
        columns = pl.ds(start + k * part.shape[1], part.shape[1])
        hidden_copies.append(
            pltpu.make_async_copy(part, ref["all_hidden"][0].at[:, columns], ref["hidden_sems"][0].at[k])
        )
        hidden_copies[-1].start()
    if len(blocks) > 1:
        stack_blocks(blocks, delta)
    token[...] = jnp.zeros_like(token)
    step = tile_of(size, 512)

    def store(i):
        at = pl.multiple_of(i * tile, tile)
        return pltpu.make_async_copy(
            ref["made_tiles"][0].at[pl.ds(at, tile), :],
            ref["grad_weight"][0].at[pl.ds(pl.multiple_of(lo + at, tile), tile), pl.ds(start, size)],
            ref["stores"][0].at[i],
        )

    def body(cut, first, i):
        rows = pl.ds(pl.multiple_of(i * tile, tile), tile)
        if weight:
            x_t = ref["x"][0][:, pl.ds(pl.multiple_of(lo + i * tile, tile), tile)].T
            for at in range(0, size, step):
                ref["made_tiles"][0][rows, at : at + step] = jnp.dot(
                    x_t, delta[:, at : at + step], preferred_element_type=f32
                ).astype(bf16)
            store(i).start()
        if inputs:
            if not loaded:
                load(i).wait()
            w_rows = pl.ds(pl.multiple_of(w_first + i * tile, tile), tile)
            value = lax.dot_general(
                delta[...], w_tiles[w_rows, :], (((1,), (1,)), ((), ())), preferred_element_type=f32
            )
            into = pl.ds(pl.multiple_of((i - first) * tile, tile), tile)
            if before:
                value = value + before[cut][:, into]
            if parts == 1:
                outs[cut][:, into] = value.astype(outs[cut].dtype)
            else:
                staged = ref["staged"][0]
                staged[...] = value.astype(bf16)
                row, col = lax.axis_index("row"), lax.axis_index("col")
                tokens = outs[0].shape[0]
                for k in range(parts):
                    at = pl.multiple_of(place_of(col ^ k, row) * tokens, tokens)
                    outs[cut * parts + k][:, into] = staged[pl.ds(at, tokens), :]

    for cut, (low, high) in enumerate(cuts):
        first, past = (low - lo) // tile, (high - lo) // tile
        if weight and UNROLL:
            for i in range(first, past):
                body(cut, first, i)
        else:
            each(past - first, lambda i: body(cut, first, first + i))
    if weight:
        each(tiles, lambda i: store(i).wait())
    for copy in hidden_copies:
        copy.wait()


def grads(
    start, cuts, blocks, dep=None, *, weight=None, loaded=None, before=None, last=False, parts=1, x=None, into=None, hidden=(), all_hidden=None
):
    hbm = pl.BlockSpec(memory_space=pl.ANY)
    size = sum(b.shape[1] for b in blocks) if len(blocks) == 1 else blocks[0].shape[1] * (len(blocks) // 6)
    tokens = blocks[0].shape[0] * (4 if len(blocks) > 1 else 1)
    features = cuts[-1][1] - cuts[0][0]
    tile = tile_of(cuts[0][1] - cuts[0][0], TILE)
    operands, outs, scratch, aliases = [], [], [], {}

    def give(name, value, spec=None):
        operands.append((name, value, spec or resident()))

    def make(name, shape, spec=None):
        outs.append((name, shape, spec or resident()))

    def carry(name, value):
        if not isinstance(value, jax.ShapeDtypeStruct):
            aliases[len(operands)] = len(outs)
            give(name + "_before", value, hbm)
        make(name, jax.ShapeDtypeStruct(value.shape, value.dtype), hbm)

    for block in blocks:
        give("block", block)
    if len(blocks) > 1:
        scratch.append(("delta", pltpu.VMEM((tokens, size), bf16)))
    tiles, sems = pltpu.VMEM((features, size), bf16), pltpu.SemaphoreType.DMA((features // tile,))
    if weight is not None or loaded is not None:
        if loaded is None:
            give("weight", weight, hbm)
            scratch += [("weight_tiles", tiles), ("loads", sems)]
        else:
            give("loaded", loaded)
        for one in before or ():
            give("before", one)
        for low, high in cuts:
            shape = jax.ShapeDtypeStruct((tokens // parts, high - low), bf16 if last else f32)
            for _ in range(parts):
                make("grad_inputs", shape)
        if parts > 1:
            scratch.append(("staged", pltpu.VMEM((tokens, tile), bf16)))
    if x is not None:
        give("x", x)
        carry("grad_weight", into)
        scratch += [("made_tiles", tiles), ("stores", sems)]
    if hidden:
        for part in hidden:
            give("hidden", part)
        carry("all_hidden", all_hidden)
        scratch.append(("hidden_sems", pltpu.SemaphoreType.DMA((len(hidden),))))
    make("token", TOKEN)
    names = [name for name, *_ in operands + outs + scratch]
    held = [shape for _, shape in scratch if not shape.dtype == sems.dtype]
    room = EXTRA + sum(math.prod(shape.shape) * 2 for shape in held) // MIB
    work = (weight is not None or loaded is not None) + (x is not None)
    return call(
        functools.partial(grads_kernel, names, start, cuts, tile),
        [value for _, value, _ in operands],
        [spec for *_, spec in operands],
        dep,
        out_specs=[spec for *_, spec in outs],
        out_shape=[shape for _, shape, _ in outs],
        scratch_shapes=[shape for _, shape in scratch],
        input_output_aliases=aliases,
        compiler_params=params(room),
        cost_estimate=cost(2 * work * tokens * features * size, 2 * work * features * size),
        name="grads",
    )


def call(kernel, operands, in_specs, dep, **options):
    count = len(operands)

    def ordered(*refs):
        kernel(*refs[:count], *refs[count + 1 :])

    if dep is None:
        return pl.pallas_call(kernel, in_specs=in_specs, **options)(*operands)
    in_specs = [*in_specs, pl.BlockSpec(memory_space=pl.ANY)]
    return pl.pallas_call(ordered, in_specs=in_specs, **options)(*operands, dep)


def combine(name, kernel, operands, outs, dep):
    vmem = pl.BlockSpec(memory_space=pltpu.VMEM)
    like = operands[0]
    moved = sum(o.size * 2 for o in operands)
    return call(
        kernel,
        operands,
        [vmem] * len(operands),
        dep,
        out_specs=[vmem] * outs,
        out_shape=[jax.ShapeDtypeStruct(like.shape, bf16)] * outs,
        compiler_params=params(16),
        cost_estimate=cost(moved, moved),
        name=name,
    )


def at_end():
    row = lax.axis_index("row")
    return (row == 0) | (row == 3)


def pick(out, at_ends, at_middles):
    end = at_end()

    @pl.when(end)
    def _():
        out[...] = at_ends[...]

    @pl.when(jnp.logical_not(end))
    def _():
        out[...] = at_middles[...]


def pass_on_kernel(a, out):
    out[...] = a[...]


def ends_in_kernel(far, mid_m, near_d, out, relay):
    pick(out, far, mid_m)
    relay[...] = near_d[...]


def copy_two_kernel(a, b, out_a, out_b):
    out_a[...] = a[...]
    out_b[...] = b[...]


def far_sum_kernel(mid, far_m, far, far_in, out, out_sum):
    pick(out, mid, far_m)
    out_sum[...] = far[...] + far_in[...]


def far_sum_only_kernel(mid, far, far_in, out, out_sum):
    out[...] = mid[...]
    out_sum[...] = far[...] + far_in[...]


def near_sum_kernel(near, far_sum, mid, mid_in, out, out_sum):
    end = at_end()
    out_sum[...] = mid[...] + mid_in[...]

    @pl.when(end)
    def _():
        out[...] = near[...]

    @pl.when(jnp.logical_not(end))
    def _():
        out[...] = near[...] + far_sum[...]


def gelu_kernel(own, near_sum, mid_sum, cotangent, hidden, delta):
    end = at_end()
    width = own.shape[1]
    step = 256 if width % 256 == 0 else width

    def body(j, carry):
        cols = pl.ds(pl.multiple_of(j * step, step), step)
        from_mid = jnp.where(end, 0.0, mid_sum[:, cols].astype(f32))
        preact = own[:, cols].astype(f32) + from_mid + near_sum[:, cols].astype(f32)
        value, slope = gelu_both(preact)
        hidden[:, cols] = value.astype(bf16)
        delta[:, cols] = (cotangent[:, cols].astype(f32) * slope).astype(bf16)
        return carry

    lax.fori_loop(0, width // step, body, 0)


def sum_kernel(a, b, c, out, relay):
    out[...] = a[...] + b[...]
    relay[...] = c[...]


def finish_kernel(*refs):
    out = refs[-1]
    width = refs[0].shape[1]
    for k in range(SPLIT):
        keep, give, across = refs[3 * k : 3 * k + 3]
        out[:, k * width : (k + 1) * width] = (
            keep[...].astype(f32) + give[...].astype(f32) + across[...].astype(f32)
        ).astype(bf16)


def join(name, kernel, operands, shape, dep):
    moved = sum(o.size * 2 for o in operands)
    return call(
        kernel,
        list(operands),
        [resident()] * len(operands),
        dep,
        grid=(1,),
        out_specs=whole(*shape),
        out_shape=jax.ShapeDtypeStruct(shape, bf16),
        compiler_params=params(16),
        cost_estimate=cost(moved, moved),
        name=name,
    )


def gather_inputs(inputs, meanwhile):
    across = send(inputs, "col", ACROSS)
    (local,) = combine("local", pass_on_kernel, (inputs,), 1, None)
    beside = send(local, "col", CORES)
    made = meanwhile(local)
    (relayed,) = combine("corner", pass_on_kernel, (across,), 1, made[0])
    corner = send(relayed, "col", CORES)
    return (local, beside, relayed, corner), made


class Order:
    def __init__(self, plan):
        self.plan, self.steps, self.token = plan, 0, None

    def between(self, name, kernel, operands, outs=2):
        values = combine(name, kernel, operands, outs, self.token)
        self.token = values[0]
        return values

    def work(self):
        for kernel in self.plan.get(self.steps, ()):
            self.token = kernel(self.token)
        self.steps += 1


def on_line(inputs, weight, cotangent):
    depth, width = weight.shape
    tokens = 4 * inputs.shape[0]
    chunks = STREAMS * ROUNDS
    size = width // chunks
    cuts = [depth * k // SPLIT for k in range(SPLIT + 1)]
    bounds = list(zip(cuts[:-1], cuts[1:]))
    sums, delta, blocks, hidden = {}, {}, {}, {}
    total = [None] * SPLIT
    state = {
        "weight": jax.ShapeDtypeStruct(weight.shape, bf16),
        "hidden": jax.ShapeDtypeStruct(cotangent.shape, bf16),
    }
    plan = {}
    order = Order(plan)

    def forward_of(k):
        def run(dep):
            following = (k + 1) * size if EARLY <= k + 1 < chunks else None
            made = forward(x, weight, k * size, size, tokens, 4, dep, loaded.get(k), following)
            if following is not None:
                *made, loaded[k + 1] = made
            *sums[k], token = made
            return token

        return run

    def grads_of(k, *which, both=True):
        def run(dep):
            more = {"weight": weight}
            if k in loaded:
                more = {"loaded": loaded[k]}
            if both:
                more |= {"x": x, "into": state["weight"]}
                if which[0] == 0:
                    more |= {"hidden": [hidden[k]], "all_hidden": state["hidden"]}
            before = [total[p] for p in which] if total[which[0]] is not None else None
            made = list(
                grads(k * size, [bounds[p] for p in which], blocks[k], dep, before=before, **more)
            )
            for p in which:
                total[p] = made.pop(0)
            if both:
                state["weight"] = made.pop(0)
                if which[0] == 0:
                    state["hidden"] = made.pop(0)
            return made.pop(0)

        return run

    def chain(mine):
        def exchange(values):
            return [send(value, PLANE, to) for value, to in zip(values, (HALVES, MIDDLE))]

        for at, k in enumerate([*mine, None]):
            before = mine[at - 1] if at else None
            if before is not None:
                own, near_sum, mid_sum = pending
                part = cotangent[:, before * size : (before + 1) * size]
                hidden[before], delta[before] = order.between(
                    "gelu", gelu_kernel, (own, near_sum, mid_sum, part)
                )
                near_d, mid_m = exchange((delta[before], delta[before]))
                order.work()
                yield
            if k is not None:
                own, near, mid, far = sums[k]
            if k is None:
                mid_e, far_m = exchange(order.between("relay", copy_two_kernel, (mid_m, near_d)))
                order.work()
                yield
                (far_e,) = exchange(order.between("relay_far", pass_on_kernel, (far_m,), 1))
            elif before is None:
                far_in = send(far, PLANE, HALVES)
                order.work()
                yield
                mid_in, far_sum = exchange(
                    order.between("far_sum", far_sum_only_kernel, (mid, far, far_in))
                )
            else:
                far_in, far_m = exchange(
                    order.between("ends_in", ends_in_kernel, (far, mid_m, near_d))
                )
                order.work()
                yield
                mid_in, far_sum = exchange(
                    order.between("far_sum", far_sum_kernel, (mid, far_m, far, far_in))
                )
                mid_e, far_e = far_in, mid_in
            if before is not None:
                blocks[before] = [delta[before], near_d, mid_m, mid_e, far_m, far_e]
            order.work()
            yield
            if k is not None:
                near_sum, mid_sum = exchange(
                    order.between("near_sum", near_sum_kernel, (near, far_sum, mid, mid_in))
                )
                pending = (own, near_sum, mid_sum)
                order.work()
                yield

    early = range(EARLY)
    pieces, made = gather_inputs(
        inputs, lambda dep: preload(weight, [k * size for k in early], size, dep)
    )
    loaded = dict(zip(early, made))
    *sums[0], order.token, x = forward(pieces, weight, 0, size, tokens, 4, None, loaded.get(0))
    plan.update(planned(forward_of, grads_of))
    chains = [chain(list(range(s, chunks, STREAMS))) for s in range(STREAMS)]
    live = list(chains)
    while live:
        for one in list(live):
            if next(one, live) is live:
                live.remove(one)

    final = chunks - 1
    for k in range(chunks - STREAMS, final):
        order.token = grads_of(k, *range(SPLIT), both=False)(order.token)
    finals, parts, far_in = [], [], []

    def across(part):
        keep, give, keep_far, _ = parts[part]
        far_sum, give = order.between("far_sum_col", sum_kernel, (keep_far, far_in[part], give))
        finals.extend([keep, send(far_sum, "col", ACROSS), send(give, "col", CORES)])

    for part, cut in enumerate(bounds):
        *pieces, order.token = grads(
            final * size,
            [cut],
            blocks[final],
            order.token,
            weight=weight,
            loaded=loaded.get(final),
            before=[total[part]],
            last=True,
            parts=4,
        )
        if part:
            across(part - 1)
        parts.append(pieces)
        far_in.append(send(pieces[3], "col", CORES))
    across(SPLIT - 1)
    late = range(chunks - STREAMS, chunks)
    grad_weight, all_hidden, order.token = grads(
        late[0] * size,
        [(0, depth)],
        [block for k in late for block in blocks[k]],
        order.token,
        x=x,
        into=state["weight"],
        hidden=[hidden[k] for k in late],
        all_hidden=state["hidden"],
    )
    grad_inputs = join("finish", finish_kernel, finals, inputs.shape, order.token)
    return (all_hidden, grad_inputs, grad_weight)


def planned(forward_of, grads_of):
    return {
        0: [forward_of(1)],
        2: [forward_of(2)],
        4: [forward_of(3)],
        12: [grads_of(0, 0)],
        14: [grads_of(0, 1)],
        16: [grads_of(1, 0)],
        18: [grads_of(1, 1)],
    }


def on_any(inputs, weight, cotangent):
    depth, width = weight.shape
    x = lax.all_gather(inputs, "col", axis=0, tiled=True)
    tokens = x.shape[0]
    sums, _ = forward(x, weight, 0, width, tokens, 1)
    preact = lax.psum_scatter(sums, "row", scatter_dimension=0, tiled=True).astype(f32)
    value, slope = gelu_both(preact)
    delta = (cotangent.astype(f32) * slope).astype(bf16)
    blocks = [lax.all_gather(delta, "row", axis=0, tiled=True)]
    made = jax.ShapeDtypeStruct(weight.shape, bf16)
    sums, grad_weight, _ = grads(0, [(0, depth)], blocks, weight=weight, last=True, x=x, into=made)
    grad_inputs = lax.psum_scatter(sums, "col", scatter_dimension=0, tiled=True)
    return (value.astype(bf16), grad_inputs, grad_weight)


def solution(mesh):
    in_specs = (P(("groups", "col"), "row"), P("row", "col"), P(("groups", "row"), "col"))
    out_specs = (
        P(("groups", "row"), "col"),
        P(("groups", "col"), "row"),
        P(("groups", "row"), "col"),
    )
    fits = mesh.shape["row"] == 4 and mesh.shape["col"] == 4
    return jax.shard_map(
        on_line if fits else on_any,
        mesh=mesh,
        in_specs=in_specs,
        out_specs=out_specs,
        check_vma=False,
    )
```

```python
import functools
import math

import jax
import jax.numpy as jnp
from jax import lax
from jax.experimental import pallas as pl
from jax.experimental.pallas import tpu as pltpu
from jax.sharding import PartitionSpec as P

tanh_scale = 0.7978845608028654
cubic_coef = 0.044715
bf16 = jnp.bfloat16
f32 = jnp.float32
MIB = 1 << 20

CORES = ((0, 1), (1, 0), (2, 3), (3, 2))
ACROSS = ((0, 2), (2, 0), (1, 3), (3, 1))
PLANE = ("row", "col")
HALVES = tuple((4 * row + col, 4 * (row ^ 1) + col) for row in range(4) for col in range(4))
MIDDLE = tuple(
    (4 * row + col, 4 * (3 - row) + col if row in (1, 2) else 4 * row + (col ^ 1))
    for row in range(4)
    for col in range(4)
)

STREAMS = 2
ROUNDS = 2
SPLIT = 2
EARLY = 2


def gelu_both(preact):
    inner = tanh_scale * (preact + cubic_coef * preact * preact * preact)
    tangent = jnp.tanh(inner)
    value = 0.5 * preact * (1.0 + tangent)
    slope = 0.5 * (1.0 + tangent) + 0.5 * preact * (1.0 - tangent * tangent) * tanh_scale * (
        1.0 + 3.0 * cubic_coef * preact * preact
    )
    return value, slope


def send(value, axis, pairs):
    return lax.ppermute(value, axis, pairs)


def place_of(token_block, row):
    same_half = (token_block // 2) == (row // 2)
    return jnp.where(same_half, token_block ^ row, jnp.where(row < 2, token_block, 3 - token_block))


def params(limit=48):
    return pltpu.CompilerParams(vmem_limit_bytes=limit * MIB)


def cost(flops, bytes_accessed):
    return pl.CostEstimate(flops=int(flops), bytes_accessed=int(bytes_accessed), transcendentals=0)


def whole(*shape):
    return pl.BlockSpec(shape, lambda j: (0,) * len(shape))


def resident():
    return pl.BlockSpec(memory_space=pltpu.VMEM)


def tile_of(size, want):
    tile = want
    while size % tile:
        tile //= 2
    return tile


TILE = 512
LOADED_TILE = 768
EXTRA = 4
UNROLL = True
TOKEN = jax.ShapeDtypeStruct((8, 128), f32)


def fetch(source, rows, columns, buffer, sems, tile, by_rows, i):
    at = pl.ds(pl.multiple_of(i * tile, tile), tile)
    if by_rows:
        part = source.at[pl.ds(pl.multiple_of(rows[0] + i * tile, tile), tile), pl.ds(*columns)]
        return pltpu.make_async_copy(part, buffer.at[at, :], sems.at[i])
    part = source.at[pl.ds(*rows), pl.ds(pl.multiple_of(columns[0] + i * tile, tile), tile)]
    return pltpu.make_async_copy(part, buffer.at[:, at], sems.at[i])


def each(count, body):
    def run(i, carry):
        body(i)
        return carry

    lax.fori_loop(0, count, run, 0)


def preload_kernel(starts, w_ref, *refs):
    *outs, sems = refs
    copies = []
    for k, (start, out) in enumerate(zip(starts, outs)):
        part = w_ref.at[:, pl.ds(start, out.shape[1])]
        copies.append(pltpu.make_async_copy(part, out, sems.at[k]))
        copies[-1].start()
    for copy in copies:
        copy.wait()


def preload(weight, starts, size, dep):
    shape = jax.ShapeDtypeStruct((weight.shape[0], size), bf16)
    return call(
        functools.partial(preload_kernel, starts),
        [weight],
        [pl.BlockSpec(memory_space=pl.ANY)],
        dep,
        out_specs=[resident()] * len(starts),
        out_shape=[shape] * len(starts),
        scratch_shapes=[pltpu.SemaphoreType.DMA((len(starts),))],
        compiler_params=params(16),
        cost_estimate=cost(0, 2 * len(starts) * shape.size),
        name="preload",
    )


def forward_kernel(start, tile, parts, first, loaded, following, w_ref, *refs):
    ahead = None
    if following is not None:
        source, *refs, made, sem = refs
        ahead = pltpu.make_async_copy(
            source.at[:, pl.ds(following, made.shape[1])], made, sem.at[0]
        )
        ahead.start()
    if loaded:
        buffer = w_ref
    else:
        *refs, buffer, sems = refs
    depth, size = buffer.shape
    if not loaded:
        load = functools.partial(fetch, w_ref, (0, depth), (start, size), buffer, sems, tile, False)
        each(size // tile, lambda i: load(i).start())
    if first:
        pieces, outs, token, x_ref = refs[:parts], refs[parts : 2 * parts], refs[-2], refs[-1]
        rows = outs[0].shape[0]
        row, col = lax.axis_index("row"), lax.axis_index("col")
        for k, piece in enumerate(pieces):
            at = pl.multiple_of(place_of(col ^ k, row) * rows, rows)
            x_ref[pl.ds(at, rows), :] = piece[...]
    else:
        x_ref, *outs, token = refs
        rows = outs[0].shape[0]
    token[...] = jnp.zeros_like(token)

    def body(i):
        columns = pl.ds(pl.multiple_of(i * tile, tile), tile)
        if not loaded:
            load(i).wait()
        sums = jnp.dot(x_ref[...], buffer[:, columns], preferred_element_type=f32).astype(bf16)
        for k, out in enumerate(outs):
            out[:, columns] = sums[k * rows : (k + 1) * rows]

    each(size // tile, body)
    if ahead is not None:
        ahead.wait()


def forward(x, weight, start, size, tokens, parts, dep=None, loaded=None, following=None):
    depth = weight.shape[0]
    tile = tile_of(size, LOADED_TILE if loaded is not None else TILE)
    rows = tokens // parts
    first = isinstance(x, tuple)
    here = loaded is not None
    operands = [loaded if here else weight, *(x if first else (x,))]
    specs = [resident() if here else pl.BlockSpec(memory_space=pl.ANY)] + [resident()] * (len(operands) - 1)
    if following is not None:
        operands.insert(1, weight)
        specs.insert(1, pl.BlockSpec(memory_space=pl.ANY))
    out_shape = [jax.ShapeDtypeStruct((rows, size), bf16)] * parts + [TOKEN]
    if first:
        out_shape.append(jax.ShapeDtypeStruct((tokens, depth), bf16))
    scratch = [] if here else [pltpu.VMEM((depth, size), bf16), pltpu.SemaphoreType.DMA((size // tile,))]
    if following is not None:
        assert here and not first
        out_shape.append(jax.ShapeDtypeStruct((depth, size), bf16))
        scratch.append(pltpu.SemaphoreType.DMA((1,)))
    return call(
        functools.partial(forward_kernel, start, tile, parts, first, here, following),
        operands,
        specs,
        dep,
        out_specs=[resident()] * len(out_shape),
        out_shape=out_shape,
        scratch_shapes=scratch,
        compiler_params=params(12 if here else 36),
        cost_estimate=cost(2 * tokens * depth * size, 2 * depth * size),
        name="forward_sums",
    )


def stack_blocks(refs, all_ref):
    rows, width = refs[0].shape
    end = at_end()
    for q in range(len(refs) // 6):
        own, near, mid_m, mid_e, far_m, far_e = refs[6 * q : 6 * q + 6]
        columns = slice(q * width, (q + 1) * width)
        all_ref[0:rows, columns] = own[...]
        all_ref[rows : 2 * rows, columns] = near[...]

        @pl.when(jnp.logical_not(end))
        def _():
            all_ref[2 * rows : 3 * rows, columns] = mid_m[...]
            all_ref[3 * rows :, columns] = far_m[...]

        @pl.when(end)
        def _():
            all_ref[2 * rows : 3 * rows, columns] = mid_e[...]
            all_ref[3 * rows :, columns] = far_e[...]


def grads_kernel(names, start, cuts, tile, *refs):
    ref = {}
    for name, one in zip(names, refs, strict=True):
        ref.setdefault(name, []).append(one)
    blocks, token = ref["block"], ref["token"][0]
    inputs, weight = "weight" in ref or "loaded" in ref, "grad_weight" in ref
    loaded = "loaded" in ref
    delta = ref["delta"][0] if len(blocks) > 1 else blocks[0]
    size = delta.shape[1]
    lo, tiles = cuts[0][0], (cuts[-1][1] - cuts[0][0]) // tile
    w_first = lo if loaded else 0
    hidden_copies = []
    if inputs:
        outs, before = ref["grad_inputs"], ref.get("before")
        w_tiles = (ref["loaded"] if loaded else ref["weight_tiles"])[0]
        parts = len(outs) // len(cuts)
    if inputs and not loaded:
        load = functools.partial(
            fetch, ref["weight"][0], (lo, tiles * tile), (start, size), w_tiles, ref["loads"][0], tile, True
        )
        each(tiles, lambda i: load(i).start())
    for k, part in enumerate(ref.get("hidden", ())):
        columns = pl.ds(start + k * part.shape[1], part.shape[1])
        hidden_copies.append(
            pltpu.make_async_copy(part, ref["all_hidden"][0].at[:, columns], ref["hidden_sems"][0].at[k])
        )
        hidden_copies[-1].start()
    if len(blocks) > 1:
        stack_blocks(blocks, delta)
    token[...] = jnp.zeros_like(token)
    step = tile_of(size, 512)

    def store(i):
        at = pl.multiple_of(i * tile, tile)
        return pltpu.make_async_copy(
            ref["made_tiles"][0].at[pl.ds(at, tile), :],
            ref["grad_weight"][0].at[pl.ds(pl.multiple_of(lo + at, tile), tile), pl.ds(start, size)],
            ref["stores"][0].at[i],
        )

    def body(cut, first, i):
        rows = pl.ds(pl.multiple_of(i * tile, tile), tile)
        if weight:
            x_t = ref["x"][0][:, pl.ds(pl.multiple_of(lo + i * tile, tile), tile)].T
            for at in range(0, size, step):
                ref["made_tiles"][0][rows, at : at + step] = jnp.dot(
                    x_t, delta[:, at : at + step], preferred_element_type=f32
                ).astype(bf16)
            store(i).start()
        if inputs:
            if not loaded:
                load(i).wait()
            w_rows = pl.ds(pl.multiple_of(w_first + i * tile, tile), tile)
            value = lax.dot_general(
                delta[...], w_tiles[w_rows, :], (((1,), (1,)), ((), ())), preferred_element_type=f32
            )
            into = pl.ds(pl.multiple_of((i - first) * tile, tile), tile)
            if before:
                value = value + before[cut][:, into]
            if parts == 1:
                outs[cut][:, into] = value.astype(outs[cut].dtype)
            else:
                staged = ref["staged"][0]
                staged[...] = value.astype(bf16)
                row, col = lax.axis_index("row"), lax.axis_index("col")
                tokens = outs[0].shape[0]
                for k in range(parts):
                    at = pl.multiple_of(place_of(col ^ k, row) * tokens, tokens)
                    outs[cut * parts + k][:, into] = staged[pl.ds(at, tokens), :]

    for cut, (low, high) in enumerate(cuts):
        first, past = (low - lo) // tile, (high - lo) // tile
        if weight and UNROLL:
            for i in range(first, past):
                body(cut, first, i)
        else:
            each(past - first, lambda i: body(cut, first, first + i))
    if weight:
        each(tiles, lambda i: store(i).wait())
    for copy in hidden_copies:
        copy.wait()


def grads(
    start, cuts, blocks, dep=None, *, weight=None, loaded=None, before=None, last=False, parts=1, x=None, into=None, hidden=(), all_hidden=None
):
    hbm = pl.BlockSpec(memory_space=pl.ANY)
    size = sum(b.shape[1] for b in blocks) if len(blocks) == 1 else blocks[0].shape[1] * (len(blocks) // 6)
    tokens = blocks[0].shape[0] * (4 if len(blocks) > 1 else 1)
    features = cuts[-1][1] - cuts[0][0]
    tile = tile_of(cuts[0][1] - cuts[0][0], LOADED_TILE if loaded is not None else TILE)
    operands, outs, scratch, aliases = [], [], [], {}

    def give(name, value, spec=None):
        operands.append((name, value, spec or resident()))

    def make(name, shape, spec=None):
        outs.append((name, shape, spec or resident()))

    def carry(name, value):
        if not isinstance(value, jax.ShapeDtypeStruct):
            aliases[len(operands)] = len(outs)
            give(name + "_before", value, hbm)
        make(name, jax.ShapeDtypeStruct(value.shape, value.dtype), hbm)

    for block in blocks:
        give("block", block)
    if len(blocks) > 1:
        scratch.append(("delta", pltpu.VMEM((tokens, size), bf16)))
    tiles, sems = pltpu.VMEM((features, size), bf16), pltpu.SemaphoreType.DMA((features // tile,))
    if weight is not None or loaded is not None:
        if loaded is None:
            give("weight", weight, hbm)
            scratch += [("weight_tiles", tiles), ("loads", sems)]
        else:
            give("loaded", loaded)
        for one in before or ():
            give("before", one)
        for low, high in cuts:
            shape = jax.ShapeDtypeStruct((tokens // parts, high - low), bf16 if last else f32)
            for _ in range(parts):
                make("grad_inputs", shape)
        if parts > 1:
            scratch.append(("staged", pltpu.VMEM((tokens, tile), bf16)))
    if x is not None:
        give("x", x)
        carry("grad_weight", into)
        scratch += [("made_tiles", tiles), ("stores", sems)]
    if hidden:
        for part in hidden:
            give("hidden", part)
        carry("all_hidden", all_hidden)
        scratch.append(("hidden_sems", pltpu.SemaphoreType.DMA((len(hidden),))))
    make("token", TOKEN)
    names = [name for name, *_ in operands + outs + scratch]
    held = [shape for _, shape in scratch if not shape.dtype == sems.dtype]
    room = EXTRA + sum(math.prod(shape.shape) * 2 for shape in held) // MIB
    work = (weight is not None or loaded is not None) + (x is not None)
    return call(
        functools.partial(grads_kernel, names, start, cuts, tile),
        [value for _, value, _ in operands],
        [spec for *_, spec in operands],
        dep,
        out_specs=[spec for *_, spec in outs],
        out_shape=[shape for _, shape, _ in outs],
        scratch_shapes=[shape for _, shape in scratch],
        input_output_aliases=aliases,
        compiler_params=params(room),
        cost_estimate=cost(2 * work * tokens * features * size, 2 * work * features * size),
        name="grads",
    )


def call(kernel, operands, in_specs, dep, **options):
    count = len(operands)

    def ordered(*refs):
        kernel(*refs[:count], *refs[count + 1 :])

    if dep is None:
        return pl.pallas_call(kernel, in_specs=in_specs, **options)(*operands)
    in_specs = [*in_specs, pl.BlockSpec(memory_space=pl.ANY)]
    return pl.pallas_call(ordered, in_specs=in_specs, **options)(*operands, dep)


def combine(name, kernel, operands, outs, dep):
    vmem = pl.BlockSpec(memory_space=pltpu.VMEM)
    like = operands[0]
    moved = sum(o.size * 2 for o in operands)
    return call(
        kernel,
        operands,
        [vmem] * len(operands),
        dep,
        out_specs=[vmem] * outs,
        out_shape=[jax.ShapeDtypeStruct(like.shape, bf16)] * outs,
        compiler_params=params(16),
        cost_estimate=cost(moved, moved),
        name=name,
    )


def at_end():
    row = lax.axis_index("row")
    return (row == 0) | (row == 3)


def pick(out, at_ends, at_middles):
    end = at_end()

    @pl.when(end)
    def _():
        out[...] = at_ends[...]

    @pl.when(jnp.logical_not(end))
    def _():
        out[...] = at_middles[...]


def pass_on_kernel(a, out):
    out[...] = a[...]


def ends_in_kernel(far, mid_m, near_d, out, relay):
    pick(out, far, mid_m)
    relay[...] = near_d[...]


def copy_two_kernel(a, b, out_a, out_b):
    out_a[...] = a[...]
    out_b[...] = b[...]


def far_sum_kernel(mid, far_m, far, far_in, out, out_sum):
    pick(out, mid, far_m)
    out_sum[...] = far[...] + far_in[...]


def far_sum_only_kernel(mid, far, far_in, out, out_sum):
    out[...] = mid[...]
    out_sum[...] = far[...] + far_in[...]


def near_sum_kernel(near, far_sum, mid, mid_in, out, out_sum):
    end = at_end()
    out_sum[...] = mid[...] + mid_in[...]

    @pl.when(end)
    def _():
        out[...] = near[...]

    @pl.when(jnp.logical_not(end))
    def _():
        out[...] = near[...] + far_sum[...]


def gelu_kernel(own, near_sum, mid_sum, cotangent, hidden, delta):
    end = at_end()
    width = own.shape[1]
    step = 256 if width % 256 == 0 else width

    def body(j, carry):
        cols = pl.ds(pl.multiple_of(j * step, step), step)
        from_mid = jnp.where(end, 0.0, mid_sum[:, cols].astype(f32))
        preact = own[:, cols].astype(f32) + from_mid + near_sum[:, cols].astype(f32)
        value, slope = gelu_both(preact)
        hidden[:, cols] = value.astype(bf16)
        delta[:, cols] = (cotangent[:, cols].astype(f32) * slope).astype(bf16)
        return carry

    lax.fori_loop(0, width // step, body, 0)


def sum_kernel(a, b, c, out, relay):
    out[...] = a[...] + b[...]
    relay[...] = c[...]


def finish_kernel(*refs):
    out = refs[-1]
    width = refs[0].shape[1]
    for k in range(SPLIT):
        keep, give, across = refs[3 * k : 3 * k + 3]
        out[:, k * width : (k + 1) * width] = (
            keep[...].astype(f32) + give[...].astype(f32) + across[...].astype(f32)
        ).astype(bf16)


def join(name, kernel, operands, shape, dep):
    moved = sum(o.size * 2 for o in operands)
    return call(
        kernel,
        list(operands),
        [resident()] * len(operands),
        dep,
        grid=(1,),
        out_specs=whole(*shape),
        out_shape=jax.ShapeDtypeStruct(shape, bf16),
        compiler_params=params(16),
        cost_estimate=cost(moved, moved),
        name=name,
    )


def gather_inputs(inputs, meanwhile):
    across = send(inputs, "col", ACROSS)
    (local,) = combine("local", pass_on_kernel, (inputs,), 1, None)
    beside = send(local, "col", CORES)
    made = meanwhile(local)
    (relayed,) = combine("corner", pass_on_kernel, (across,), 1, made[0])
    corner = send(relayed, "col", CORES)
    return (local, beside, relayed, corner), made


class Order:
    def __init__(self, plan):
        self.plan, self.steps, self.token = plan, 0, None

    def between(self, name, kernel, operands, outs=2):
        values = combine(name, kernel, operands, outs, self.token)
        self.token = values[0]
        return values

    def work(self):
        for kernel in self.plan.get(self.steps, ()):
            self.token = kernel(self.token)
        self.steps += 1


def on_line(inputs, weight, cotangent):
    depth, width = weight.shape
    tokens = 4 * inputs.shape[0]
    chunks = STREAMS * ROUNDS
    size = width // chunks
    cuts = [depth * k // SPLIT for k in range(SPLIT + 1)]
    bounds = list(zip(cuts[:-1], cuts[1:]))
    sums, delta, blocks, hidden = {}, {}, {}, {}
    total = [None] * SPLIT
    state = {
        "weight": jax.ShapeDtypeStruct(weight.shape, bf16),
        "hidden": jax.ShapeDtypeStruct(cotangent.shape, bf16),
    }
    plan = {}
    order = Order(plan)

    def forward_of(k):
        def run(dep):
            following = (k + 1) * size if EARLY <= k + 1 < chunks else None
            made = forward(x, weight, k * size, size, tokens, 4, dep, loaded.get(k), following)
            if following is not None:
                *made, loaded[k + 1] = made
            *sums[k], token = made
            return token

        return run

    def grads_of(k, *which, both=True):
        def run(dep):
            more = {"weight": weight}
            if k in loaded:
                more = {"loaded": loaded[k]}
            if both:
                more |= {"x": x, "into": state["weight"]}
                if which[0] == 0:
                    more |= {"hidden": [hidden[k]], "all_hidden": state["hidden"]}
            before = [total[p] for p in which] if total[which[0]] is not None else None
            made = list(
                grads(k * size, [bounds[p] for p in which], blocks[k], dep, before=before, **more)
            )
            for p in which:
                total[p] = made.pop(0)
            if both:
                state["weight"] = made.pop(0)
                if which[0] == 0:
                    state["hidden"] = made.pop(0)
            return made.pop(0)

        return run

    def chain(mine):
        def exchange(values):
            return [send(value, PLANE, to) for value, to in zip(values, (HALVES, MIDDLE))]

        for at, k in enumerate([*mine, None]):
            before = mine[at - 1] if at else None
            if before is not None:
                own, near_sum, mid_sum = pending
                part = cotangent[:, before * size : (before + 1) * size]
                hidden[before], delta[before] = order.between(
                    "gelu", gelu_kernel, (own, near_sum, mid_sum, part)
                )
                near_d, mid_m = exchange((delta[before], delta[before]))
                order.work()
                yield
            if k is not None:
                own, near, mid, far = sums[k]
            if k is None:
                mid_e, far_m = exchange(order.between("relay", copy_two_kernel, (mid_m, near_d)))
                order.work()
                yield
                (far_e,) = exchange(order.between("relay_far", pass_on_kernel, (far_m,), 1))
            elif before is None:
                far_in = send(far, PLANE, HALVES)
                order.work()
                yield
                mid_in, far_sum = exchange(
                    order.between("far_sum", far_sum_only_kernel, (mid, far, far_in))
                )
            else:
                far_in, far_m = exchange(
                    order.between("ends_in", ends_in_kernel, (far, mid_m, near_d))
                )
                order.work()
                yield
                mid_in, far_sum = exchange(
                    order.between("far_sum", far_sum_kernel, (mid, far_m, far, far_in))
                )
                mid_e, far_e = far_in, mid_in
            if before is not None:
                blocks[before] = [delta[before], near_d, mid_m, mid_e, far_m, far_e]
            order.work()
            yield
            if k is not None:
                near_sum, mid_sum = exchange(
                    order.between("near_sum", near_sum_kernel, (near, far_sum, mid, mid_in))
                )
                pending = (own, near_sum, mid_sum)
                order.work()
                yield

    early = range(EARLY)
    pieces, made = gather_inputs(
        inputs, lambda dep: preload(weight, [k * size for k in early], size, dep)
    )
    loaded = dict(zip(early, made))
    *sums[0], order.token, x = forward(pieces, weight, 0, size, tokens, 4, None, loaded.get(0))
    plan.update(planned(forward_of, grads_of))
    chains = [chain(list(range(s, chunks, STREAMS))) for s in range(STREAMS)]
    live = list(chains)
    while live:
        for one in list(live):
            if next(one, live) is live:
                live.remove(one)

    final = chunks - 1
    for k in range(chunks - STREAMS, final):
        order.token = grads_of(k, *range(SPLIT), both=False)(order.token)
    finals, parts, far_in = [], [], []

    def across(part):
        keep, give, keep_far, _ = parts[part]
        far_sum, give = order.between("far_sum_col", sum_kernel, (keep_far, far_in[part], give))
        finals.extend([keep, send(far_sum, "col", ACROSS), send(give, "col", CORES)])

    for part, cut in enumerate(bounds):
        *pieces, order.token = grads(
            final * size,
            [cut],
            blocks[final],
            order.token,
            weight=weight,
            loaded=loaded.get(final),
            before=[total[part]],
            last=True,
            parts=4,
        )
        if part:
            across(part - 1)
        parts.append(pieces)
        far_in.append(send(pieces[3], "col", CORES))
    across(SPLIT - 1)
    late = range(chunks - STREAMS, chunks)
    grad_weight, all_hidden, order.token = grads(
        late[0] * size,
        [(0, depth)],
        [block for k in late for block in blocks[k]],
        order.token,
        x=x,
        into=state["weight"],
        hidden=[hidden[k] for k in late],
        all_hidden=state["hidden"],
    )
    grad_inputs = join("finish", finish_kernel, finals, inputs.shape, order.token)
    return (all_hidden, grad_inputs, grad_weight)


def planned(forward_of, grads_of):
    return {
        0: [forward_of(1)],
        2: [forward_of(2)],
        4: [forward_of(3)],
        12: [grads_of(0, 0)],
        14: [grads_of(0, 1)],
        16: [grads_of(1, 0)],
        18: [grads_of(1, 1)],
    }


def on_any(inputs, weight, cotangent):
    depth, width = weight.shape
    x = lax.all_gather(inputs, "col", axis=0, tiled=True)
    tokens = x.shape[0]
    sums, _ = forward(x, weight, 0, width, tokens, 1)
    preact = lax.psum_scatter(sums, "row", scatter_dimension=0, tiled=True).astype(f32)
    value, slope = gelu_both(preact)
    delta = (cotangent.astype(f32) * slope).astype(bf16)
    blocks = [lax.all_gather(delta, "row", axis=0, tiled=True)]
    made = jax.ShapeDtypeStruct(weight.shape, bf16)
    sums, grad_weight, _ = grads(0, [(0, depth)], blocks, weight=weight, last=True, x=x, into=made)
    grad_inputs = lax.psum_scatter(sums, "col", scatter_dimension=0, tiled=True)
    return (value.astype(bf16), grad_inputs, grad_weight)


def solution(mesh):
    in_specs = (P(("groups", "col"), "row"), P("row", "col"), P(("groups", "row"), "col"))
    out_specs = (
        P(("groups", "row"), "col"),
        P(("groups", "col"), "row"),
        P(("groups", "row"), "col"),
    )
    fits = mesh.shape["row"] == 4 and mesh.shape["col"] == 4
    return jax.shard_map(
        on_line if fits else on_any,
        mesh=mesh,
        in_specs=in_specs,
        out_specs=out_specs,
        check_vma=False,
    )
```
